32 devices in a mesh: scan: 2 (over x), tile: 4 (over y, core), mode: 4 (over z).
Axes of the slice: x: 2, y: 2, z: 4, core: 2. Of those that a mesh axis runs over, the one named last changes fastest.
Arguments:
- object_field: float32 [8, 4, 16, 2, 384], P(None, 'tile'), may hold values from -6 to 6
- probe_modes: float32 [4, 256, 512], P('mode'), may hold values from -6 to 6
- intensities: float32 [8, 256, 256], P(('scan', 'tile')), may hold values from 0.1 to 4
- positions: int32 [8, 2], replicated, may hold values from 0 to 256, as said below
Outputs:
- new_object: float32 [8, 4, 16, 2, 384], P(None, 'tile')
- new_probe: float32 [4, 256, 512], P('mode')
The draws below stay inside these ranges and needn't reach their ends.
Inputs may be any that keep to these rules, and one draw needn't show every extreme that they name: Row positions are multiples of 16; every window of 256 x 256 lies inside the object. Pattern 0 has the largest row and column corner, pattern 1 the corner (0, 0).
All inputs are finite; a program needn't handle non-finite values.
Results may differ from the reference program's by a relative error of at most 0.0003.
Values sent between devices are 32-bit elements; how exact they have to be, the bound alone decides.
A program may use at most 64 MiB of HBM per device.

```python
import math
import jax
import jax.numpy as jnp
from jax import lax

W = 256
BLK = 16
CYCLES = 8
COLS = 384
ITERS = 1
MODES = 4
PATTERNS = 8
N_TILE = 4


def draw_positions(key, part):
    key = jax.random.fold_in(key, 7)
    row_key, col_key = jax.random.split(key)
    row_slots = (CYCLES * N_TILE * BLK - W) // BLK + 1
    row_values = jax.random.randint(row_key, (PATTERNS,), 0, row_slots) * BLK
    col_values = jax.random.randint(col_key, (PATTERNS,), 0, COLS - W + 1)
    row_values = row_values.at[0].set((row_slots - 1) * BLK).at[1].set(0)
    col_values = col_values.at[0].set(COLS - W).at[1].set(0)
    return jnp.stack([row_values, col_values], axis=1).astype(jnp.int32)


def steps_of(own_key, dims, shards, least, top_value):
    loudness = 1.0
    for position, blocks in shards:
        steps = jax.random.uniform(jax.random.fold_in(jax.random.fold_in(own_key, 6), position), (blocks,), jnp.float32, least / len(shards), top_value / len(shards))
        loudness = loudness * jnp.repeat(jnp.exp(steps), dims[position] // blocks).reshape((-1,) + (1,) * (len(dims) - 1 - position))
    return loudness


def bell_draw(key, extent, scale, bound, pieces=(), kind=jnp.bfloat16):
    drawn = jax.random.normal(key, extent, jnp.float32) * scale
    if len(pieces) > 0:
        drawn = steps_of(key, extent, pieces, -0.22, 0.18) * drawn
    return jnp.clip(drawn, min=-bound, max=bound).astype(kind)


def setup_inputs(seed: int = 0) -> dict:
    key_of = jax.random.split(jax.random.key(seed), 5)
    return {
        "object_field": bell_draw(key_of[0], (CYCLES, N_TILE, BLK, 2, COLS), 0.7, 6.0, ((1, 4),), jnp.float32),
        "probe_modes": bell_draw(key_of[1], (MODES, W, 2 * W), 0.5, 6.0, ((0, 4),), jnp.float32),
        "intensities": jnp.clip(jnp.exp(math.log(4.0) - 3.6888794 * jax.random.uniform(key_of[2], (PATTERNS, W, W), jnp.float32) ** steps_of(key_of[2], (PATTERNS, W, W), ((0, 8),), -0.2, 0.2)), 0.1, 4.0),
        "positions": draw_positions(jax.random.fold_in(key_of[4], 71), 0),
    }


floor_level = 0.1
damping = 1.0

def reference(object_field, probe_modes, intensities, positions):
    width = probe_modes.shape[1]
    rows_total = object_field.shape[0] * object_field.shape[1] * object_field.shape[2]
    columns = object_field.shape[4]
    flat = object_field.reshape(rows_total, 2, columns)
    current = flat[:, 0, :] + 1j * flat[:, 1, :]
    probes = probe_modes[:, :, :width] + 1j * probe_modes[:, :, width:]
    real_type = flat.dtype
    for step in range(ITERS):

        def accumulate(carried, index):
            numerator, weight, probe_numerator, probe_weight = carried
            row_start = positions[index, 0].astype(jnp.int32)
            col_start = positions[index, 1].astype(jnp.int32)
            window = lax.dynamic_slice(current, (row_start, col_start), (width, width))
            exit_waves = probes * window[None]
            far_field = jnp.fft.fft2(exit_waves, norm='ortho')
            total_power = lax.optimization_barrier(jnp.sum(far_field.real ** 2 + far_field.imag ** 2, axis=0))
            ratio_map = jnp.sqrt(intensities[index] / jnp.maximum(total_power, floor_level))
            difference = jnp.fft.ifft2(far_field * ratio_map[None], norm='ortho') - exit_waves
            object_term = lax.optimization_barrier(jnp.sum(jnp.conj(probes) * difference, axis=0))
            object_weight = lax.optimization_barrier(jnp.sum(probes.real ** 2 + probes.imag ** 2, axis=0))
            old_terms = lax.dynamic_slice(numerator, (row_start, col_start), (width, width))
            numerator = lax.dynamic_update_slice(numerator, old_terms + object_term, (row_start, col_start))
            old_weight = lax.dynamic_slice(weight, (row_start, col_start), (width, width))
            weight = lax.dynamic_update_slice(weight, old_weight + object_weight, (row_start, col_start))
            probe_numerator = probe_numerator + jnp.conj(window)[None] * difference
            probe_weight = probe_weight + window.real ** 2 + window.imag ** 2
            return ((numerator, weight, probe_numerator, probe_weight), None)
        initial = (jnp.zeros_like(current), jnp.zeros(current.shape, real_type), jnp.zeros_like(probes), jnp.zeros((width, width), real_type))
        totals, unused = lax.scan(accumulate, initial, jnp.arange(positions.shape[0], dtype=jnp.int32))
        numerator, weight, probe_numerator, probe_weight = totals
        current = current + numerator / (weight + damping)
        probes = probes + probe_numerator / probe_weight[None]
    new_object = jnp.stack([current.real, current.imag], axis=1).reshape(object_field.shape)
    new_probe = jnp.concatenate([probes.real, probes.imag], axis=-1)
    return (new_object, new_probe)
```

```python
import functools
import math

import jax
import jax.numpy as jnp
import ml_dtypes
import numpy as np
from jax import lax
from jax.experimental import pallas as pl
from jax.experimental.pallas import tpu as pltpu
from jax.sharding import PartitionSpec as P

floor_level = 0.1
damping = 1.0
highest = lax.Precision.HIGHEST


def transform_tables(width):
    index = jnp.arange(width, dtype=jnp.int32)
    phase = (index[:, None] * index[None, :] % width).astype(jnp.float32)
    angle = phase * (2.0 * math.pi / width)
    cosine = jnp.cos(angle) / math.sqrt(width)
    sine = -jnp.sin(angle) / math.sqrt(width)
    forward_rows = jnp.block([[cosine, sine], [-sine, cosine]])
    inverse_rows = jnp.block([[cosine, -sine], [sine, cosine]])
    return (cosine, sine, forward_rows, inverse_rows)


def times(left, right):
    half = left.shape[-1] // 2
    return jnp.concatenate(
        [
            left[..., :half] * right[..., :half] - left[..., half:] * right[..., half:],
            left[..., :half] * right[..., half:] + left[..., half:] * right[..., :half],
        ],
        -1,
    )


def conj_times(left, right):
    half = left.shape[-1] // 2
    return jnp.concatenate(
        [
            left[..., :half] * right[..., :half] + left[..., half:] * right[..., half:],
            left[..., :half] * right[..., half:] - left[..., half:] * right[..., :half],
        ],
        -1,
    )


def power(values):
    half = values.shape[-1] // 2
    return values[..., :half] ** 2 + values[..., half:] ** 2


def columns_forward(cosine, sine, data):
    half = data.shape[-1] // 2
    first = jnp.einsum("ab,pbc->pac", cosine, data, precision=highest)
    second = jnp.einsum("ab,pbc->pac", sine, data, precision=highest)
    return jnp.concatenate(
        [first[..., :half] - second[..., half:], first[..., half:] + second[..., :half]], -1
    )


def columns_inverse(cosine, sine, data):
    half = data.shape[-1] // 2
    first = jnp.einsum("ab,pbc->pac", cosine, data, precision=highest)
    second = jnp.einsum("ab,pbc->pac", sine, data, precision=highest)
    return jnp.concatenate(
        [first[..., :half] + second[..., half:], first[..., half:] - second[..., :half]], -1
    )


def project(cosine, sine, spectra, intensities):
    far_field = columns_forward(cosine, sine, spectra)
    total_power = lax.psum(power(far_field), "mode")
    ratio_map = jnp.sqrt(intensities / jnp.maximum(total_power, floor_level))
    return columns_inverse(cosine, sine, far_field * jnp.concatenate([ratio_map, ratio_map], -1))


def pick_rows(rows, picks):
    return rows[picks]


def assemble(received, order):
    moved = jnp.swapaxes(received, 0, 1)
    picked = jax.vmap(pick_rows)(moved, order)
    ordered = jnp.swapaxes(picked, 1, 2)
    return ordered.reshape(ordered.shape[0], -1, ordered.shape[-1])


def disassemble(ordered, order):
    moved = jnp.swapaxes(ordered, 1, 2)
    picked = jax.vmap(pick_rows)(moved, order)
    return jnp.swapaxes(picked, 0, 1)


def place(cycle_flat, col_flat, terms, weights, shape):
    cycle_count, block, columns = shape
    count, rows, doubled = terms.shape
    width = doubled // 2
    span = jnp.arange(width, dtype=jnp.int32)
    split_terms = terms.reshape(count, rows, 2, width)
    numerator = jnp.zeros((cycle_count, block, 2, columns), jnp.float32)
    numerator = numerator.at[
        cycle_flat[:, None, None, None],
        jnp.arange(rows, dtype=jnp.int32)[None, :, None, None],
        jnp.arange(2, dtype=jnp.int32)[None, None, :, None],
        col_flat[:, None, None, None] + span,
    ].add(split_terms)
    weight = jnp.zeros((cycle_count, block, columns), jnp.float32)
    weight = weight.at[
        cycle_flat[:, None, None],
        jnp.arange(block, dtype=jnp.int32)[None, :, None],
        col_flat[:, None, None] + span,
    ].add(weights)
    return (numerator, weight)


def on_device(object_field, probe_modes, intensities, positions):
    width = probe_modes.shape[1]
    cycles = object_field.shape[0]
    block = object_field.shape[2]
    columns = object_field.shape[4]
    tiles = lax.axis_size("tile")
    patterns = intensities.shape[0]
    blocks = width // block
    rounds = blocks // tiles
    scan_index = lax.axis_index("scan")
    tile_index = lax.axis_index("tile")
    group = lax.dynamic_slice_in_dim(
        positions, scan_index * (tiles * patterns), tiles * patterns, 0
    )
    group = group.reshape(tiles, patterns, 2)
    start_blocks = group[:, :, 0] // block
    start_cols = group[:, :, 1]
    own_starts = lax.dynamic_index_in_dim(start_blocks, tile_index, 0, keepdims=False)
    first_block = jnp.mod(tile_index - start_blocks, tiles)
    patch_blocks = first_block[:, :, None] + tiles * jnp.arange(rounds, dtype=jnp.int32)
    cycle_flat = ((start_blocks[:, :, None] + patch_blocks) // tiles).reshape(-1)
    col_flat = jnp.broadcast_to(start_cols[:, :, None], patch_blocks.shape).reshape(-1)
    patch_flat = patch_blocks.reshape(-1)
    count = patch_flat.shape[0]
    lanes = jnp.arange(tiles, dtype=jnp.int32)
    gather_order = jnp.mod(lanes[None, :] + own_starts[:, None], tiles)
    scatter_order = jnp.mod(lanes[None, :] - own_starts[:, None], tiles)
    cosine, sine, forward_rows, inverse_rows = transform_tables(width)
    selector = (patch_flat[None, :] == jnp.arange(blocks, dtype=jnp.int32)[:, None]).astype(
        jnp.float32
    )
    current = object_field[:, 0]
    probe_now = probe_modes[0]

    def cut(cycle, column):
        piece = lax.dynamic_slice(current, (cycle, 0, 0, column), (1, block, 2, width))
        return piece.reshape(block, 2 * width)

    object_rows = jax.vmap(cut)(cycle_flat, col_flat)
    probe_rows = probe_now.reshape(blocks, block, 2 * width)[patch_flat]
    exit_rows = times(probe_rows, object_rows)
    spectra = jnp.dot(exit_rows.reshape(-1, 2 * width), forward_rows, precision=highest)
    arrived = lax.all_to_all(
        spectra.reshape(tiles, patterns, rounds, block, 2 * width),
        "tile",
        split_axis=0,
        concat_axis=0,
        tiled=True,
    )
    returned = project(cosine, sine, assemble(arrived, gather_order), intensities)
    outgoing = disassemble(
        returned.reshape(patterns, rounds, tiles, block, 2 * width), scatter_order
    )
    came_back = lax.all_to_all(outgoing, "tile", split_axis=0, concat_axis=0, tiled=True)
    new_rows = jnp.dot(came_back.reshape(-1, 2 * width), inverse_rows, precision=highest)
    difference = new_rows.reshape(count, block, 2 * width) - exit_rows
    terms = conj_times(probe_rows, difference)
    mixed = jnp.concatenate([conj_times(object_rows, difference), power(object_rows)], -1)
    probe_stats = jnp.dot(selector, mixed.reshape(count, -1), precision=highest).reshape(
        width, 3 * width
    )
    numerator, weight = place(
        cycle_flat, col_flat, terms, power(probe_rows), (cycles, block, columns)
    )
    numerator, weight = lax.psum((numerator, weight), ("scan", "mode"))
    summed = lax.psum(probe_stats, ("scan", "tile"))
    divisor = summed[:, 2 * width :]
    probe_next = probe_now + summed[:, : 2 * width] / jnp.concatenate([divisor, divisor], -1)
    current = current + numerator / (weight[:, :, None, :] + damping)
    return (current[:, None], probe_next[None])


MESH = pl.DeviceIdType.MESH
VMEM = pl.BlockSpec(memory_space=pltpu.VMEM)
SMEM = pl.BlockSpec(memory_space=pltpu.SMEM)
vmem_bytes = 40 * 1024 * 1024
f32 = jnp.float32


def split_tables(width):
    index = np.arange(width)
    angle = (index[:, None] * index[None, :] % width) * (2.0 * math.pi / width)
    cosine = np.cos(angle) / math.sqrt(width)
    sine = -np.sin(angle) / math.sqrt(width)
    right = np.block([[cosine, sine], [-sine, cosine]])
    parts = []
    for table in (right, right.T):
        high = table.astype(ml_dtypes.bfloat16)
        low = (table - high.astype(np.float64)).astype(ml_dtypes.bfloat16)
        parts += [high, low]
    return parts


def halves(values):
    high = values.astype(jnp.bfloat16)
    return high, (values - high.astype(f32)).astype(jnp.bfloat16)


def dot(left, right):
    return jnp.dot(left, right, preferred_element_type=f32)


def right_product(values, high_table, low_table):
    high, low = halves(values)
    return dot(high, high_table) + (dot(low, high_table) + dot(high, low_table))


def left_product(high_table, low_table, values):
    half = values.shape[-1] // 2
    high, low = halves(jnp.concatenate([values[:, :half], values[:, half:]], 0))
    out = dot(high_table, high) + (dot(high_table, low) + dot(low_table, high))
    rows = out.shape[0] // 2
    return jnp.concatenate([out[:rows], out[rows:]], 1)


def sends(me, count, id_of, src_of, dst, send, recv):
    copies = []
    for step in range(1, count):
        peer = lax.rem(me + step, count)
        copies.append(
            pltpu.make_async_remote_copy(
                src_ref=src_of(peer),
                dst_ref=dst.at[me],
                send_sem=send.at[step - 1],
                recv_sem=recv.at[step - 1],
                device_id=id_of(peer),
                device_id_type=MESH,
            )
        )
    for copy in copies:
        copy.start()
    return copies


def greet(groups):
    barrier = pltpu.get_barrier_semaphore()
    total = 0
    for me, count, id_of in groups:
        for step in range(1, count):
            pl.semaphore_signal(
                barrier, inc=1, device_id=id_of(lax.rem(me + step, count)), device_id_type=MESH
            )
            total += 1
    pl.semaphore_wait(barrier, total)


def tile_id(peer):
    return {"tile": peer}


def mode_id(peer):
    return {"mode": peer}


def pattern_id(tiles, peer):
    return {"scan": peer // tiles, "tile": lax.rem(peer, tiles)}


def any_id(tiles, modes, peer):
    return {
        "scan": peer // (tiles * modes),
        "tile": lax.rem(peer // modes, tiles),
        "mode": lax.rem(peer, modes),
    }


def fetch_kernel(sizes, rows_ref, square_ref, got_ref, squares_ref, send, recv, send_p, recv_p):
    scans, tiles, modes = sizes
    tile, mode = lax.axis_index("tile"), lax.axis_index("mode")
    greet([(tile, tiles, tile_id), (mode, modes, mode_id)])
    copies = sends(tile, tiles, tile_id, lambda peer: rows_ref.at[peer], got_ref, send, recv)
    copies += sends(mode, modes, mode_id, lambda peer: square_ref, squares_ref, send_p, recv_p)
    got_ref[tile] = rows_ref[tile]
    squares_ref[mode] = square_ref[...]
    for copy in copies:
        copy.wait()


def forward_kernel(
    tiles, place_ref, got_ref, squares_ref, probe_ref, rh, rl, gh, gl,
    window_ref, far_ref, power_ref, square_ref,
):
    width = probe_ref.shape[0]
    block = got_ref.shape[3]
    columns = got_ref.shape[4]
    start, col = place_ref[0], place_ref[1]
    shift = lax.rem(columns - col, columns)
    for index in range(width // block):
        owner = lax.rem(start + index, tiles)
        for part in range(2):
            piece = got_ref[owner, index // tiles, part]
            window_ref[index * block : (index + 1) * block, part * width : (part + 1) * width] = (
                pltpu.roll(piece, shift, 1)[:, :width]
            )
    waves = times(probe_ref[...], window_ref[...])
    far = left_product(gh[...], gl[...], right_product(waves, rh[...], rl[...]))
    far_ref[...] = far
    power_ref[...] = power(far)
    square_ref[...] = jnp.sum(squares_ref[...], axis=0)


def ratio_kernel(
    sizes, power_ref, square_ref, measured_ref, ratio_ref, squares_ref,
    got, send, recv, send_r, recv_r, send_p, recv_p,
):
    scans, tiles, modes = sizes
    mode = lax.axis_index("mode")
    me = lax.axis_index("scan") * tiles + lax.axis_index("tile")
    id_of = functools.partial(pattern_id, tiles)
    greet([(mode, modes, mode_id), (me, scans * tiles, id_of)])
    first = sends(mode, modes, mode_id, lambda peer: power_ref.at[peer], got, send, recv)
    other = sends(me, scans * tiles, id_of, lambda peer: square_ref, squares_ref, send_p, recv_p)
    got[mode] = power_ref[mode]
    squares_ref[me] = square_ref[...]
    for copy in first:
        copy.wait()
    total = got[0]
    for index in range(1, modes):
        total = total + got[index]
    ratio_ref[mode] = jnp.sqrt(measured_ref[mode] / jnp.maximum(total, floor_level))
    last = sends(
        mode, modes, mode_id, lambda peer: ratio_ref.at[mode], ratio_ref, send_r, recv_r
    )
    for copy in last + other:
        copy.wait()


def inverse_kernel(
    tiles, place_ref, ratio_ref, far_ref, window_ref, probe_ref, rh, rl, gh, gl,
    terms_ref, mixed_ref,
):
    width = probe_ref.shape[0]
    block = terms_ref.shape[2]
    start = place_ref[0]
    ratio = ratio_ref[...]
    scaled = far_ref[...] * jnp.concatenate([ratio, ratio], 1)
    waves = left_product(rh[...], rl[...], right_product(scaled, gh[...], gl[...]))
    probe, window = probe_ref[...], window_ref[...]
    difference = waves - times(probe, window)
    terms = conj_times(probe, difference)
    for index in range(width // block):
        owner = lax.rem(start + index, tiles)
        terms_ref[owner, index // tiles] = terms[index * block : (index + 1) * block]
    mixed_ref[...] = jnp.concatenate([conj_times(window, difference), power(window)], 1)


def reduce_kernel(
    sizes, terms_ref, mixed_ref, probe_ref, all_ref, next_ref,
    got, got_p, summed,
    send, recv, send_m, recv_m, send_b, recv_b, send_n, recv_n,
):
    scans, tiles, modes = sizes
    width2 = probe_ref.shape[-1]
    count = scans * tiles
    scan, tile, mode = lax.axis_index("scan"), lax.axis_index("tile"), lax.axis_index("mode")
    me = scan * tiles + tile
    id_of = functools.partial(pattern_id, tiles)
    greet([(me * modes + mode, count * modes, functools.partial(any_id, tiles, modes))])
    first = sends(mode, modes, mode_id, lambda peer: terms_ref.at[peer], got, send, recv)
    second = sends(me, count, id_of, lambda peer: mixed_ref.at[peer], got_p, send_m, recv_m)
    got[mode] = terms_ref[mode]
    got_p[me] = mixed_ref[me]
    for copy in first:
        copy.wait()
    total = got[0]
    for index in range(1, modes):
        total = total + got[index]
    summed[...] = total
    mine = tile == mode
    copies = []
    for scan_step in range(scans):
        for mode_step in range(modes):
            slot = scan_step * modes + mode_step
            copy = pltpu.make_async_remote_copy(
                src_ref=summed,
                dst_ref=all_ref.at[me],
                send_sem=send_b.at[slot],
                recv_sem=recv_b.at[me],
                device_id={
                    "scan": lax.rem(scan + scan_step, scans),
                    "tile": mode,
                    "mode": lax.rem(mode + mode_step, modes),
                },
                device_id_type=MESH,
            )
            copies.append(copy)
            if slot == 0:
                pl.when(jnp.logical_not(mine))(copy.start)
            else:
                copy.start()

    @pl.when(mine)
    def _():
        all_ref[me] = summed[...]

    for copy in second:
        copy.wait()
    totals = got_p[0]
    for index in range(1, count):
        totals = totals + got_p[index]
    divisor = totals[:, width2:]
    next_ref[me] = probe_ref[me] + totals[:, :width2] / jnp.concatenate([divisor, divisor], 1)
    last = sends(me, count, id_of, lambda peer: next_ref.at[me], next_ref, send_n, recv_n)
    for slot, copy in enumerate(copies):
        if slot == 0:
            pl.when(jnp.logical_not(mine))(copy.wait_send)
        else:
            copy.wait_send()
    for source in range(count):

        def arrived(source=source):
            pltpu.make_async_remote_copy(
                src_ref=summed,
                dst_ref=all_ref.at[source],
                send_sem=send_b.at[0],
                recv_sem=recv_b.at[source],
                device_id={"mode": mode},
                device_id_type=MESH,
            ).wait_recv()

        pl.when(jnp.logical_not(jnp.logical_and(mine, me == source)))(arrived)
    for copy in last:
        copy.wait()


def update_kernel(tiles, places_ref, all_ref, square_ref, object_ref, out_ref, weight):
    count, rounds, block, width2 = all_ref.shape
    width = width2 // 2
    columns = object_ref.shape[-1]
    tile = places_ref[count, 0]
    out_ref[...] = jnp.zeros_like(out_ref)
    weight[...] = jnp.zeros_like(weight)
    blank = jnp.zeros((block, columns - width), f32)

    def add(pattern, carry):
        start, col = places_ref[pattern, 0], places_ref[pattern, 1]
        offset = lax.rem(tile - start + tiles * block * block, tiles)
        cycle = (start + offset) // tiles
        for index in range(rounds):
            for part in range(2):
                piece = all_ref[pattern, index, :, part * width : (part + 1) * width]
                out_ref[cycle + index, part] += pltpu.roll(
                    jnp.concatenate([piece, blank], 1), col, 1
                )
            weight[cycle + index] += pltpu.roll(
                jnp.concatenate([square_ref[offset + tiles * index], blank], 1), col, 1
            )
        return carry

    lax.fori_loop(0, count, add, 0)
    divisor = weight[...] + damping
    for part in range(2):
        out_ref[:, part] = object_ref[:, part] + out_ref[:, part] / divisor


def shape(*dims):
    return jax.ShapeDtypeStruct(dims, f32)


def dma(count):
    return pltpu.SemaphoreType.DMA((count,))


def local(kernel, in_specs, outs, scratch=()):
    return pl.pallas_call(
        kernel,
        out_shape=outs,
        in_specs=in_specs,
        out_specs=jax.tree.map(lambda _: VMEM, outs),
        scratch_shapes=list(scratch),
        compiler_params=pltpu.CompilerParams(vmem_limit_bytes=vmem_bytes),
    )


def remote(kernel, number, inputs, outs, scratch):
    return pl.pallas_call(
        kernel,
        out_shape=outs,
        in_specs=[VMEM] * inputs,
        out_specs=[VMEM] * len(outs),
        scratch_shapes=scratch,
        compiler_params=pltpu.CompilerParams(
            collective_id=number, has_side_effects=True, vmem_limit_bytes=vmem_bytes
        ),
    )


def one_wave(sizes, tables, object_field, probe_modes, intensities, positions):
    scans, tiles, modes = sizes
    count = scans * tiles
    width = probe_modes.shape[1]
    cycles, _, block, _, columns = object_field.shape
    blocks = width // block
    rounds = blocks // tiles
    share = width // count
    quarter = width // modes
    scan, tile = lax.axis_index("scan"), lax.axis_index("tile")
    me = scan * tiles + tile
    starts = positions[:, 0] // block
    places = jnp.stack([starts, positions[:, 1]], 1)
    place_now = lax.dynamic_index_in_dim(places, me, 0, keepdims=False)
    probe = probe_modes[0]
    planar = jnp.swapaxes(object_field[:, 0], 1, 2)
    group = lax.dynamic_slice_in_dim(starts, scan * tiles, tiles, 0)
    first_cycle = (group + jnp.mod(tile - group, tiles)) // tiles
    rows = jnp.stack(
        [
            lax.dynamic_slice_in_dim(planar, first_cycle[index], rounds, 0)
            for index in range(tiles)
        ]
    )
    square = power(lax.dynamic_slice_in_dim(probe, me * share, share, 0))
    got, squares = remote(
        functools.partial(fetch_kernel, sizes),
        0,
        2,
        [shape(tiles, rounds, 2, block, columns), shape(modes, share, width)],
        [dma(tiles - 1), dma(tiles - 1), dma(modes - 1), dma(modes - 1)],
    )(rows, square)
    window, far, strength, square = local(
        functools.partial(forward_kernel, tiles),
        [SMEM] + [VMEM] * 7,
        [
            shape(width, 2 * width),
            shape(width, 2 * width),
            shape(width, width),
            shape(share, width),
        ],
    )(place_now, got, squares, probe, *tables)
    ratio, squares = remote(
        functools.partial(ratio_kernel, sizes),
        1,
        3,
        [shape(modes, quarter, width), shape(count, share, width)],
        [pltpu.VMEM((modes, quarter, width), f32)]
        + [dma(modes - 1)] * 4
        + [dma(count - 1)] * 2,
    )(
        strength.reshape(modes, quarter, width),
        square,
        intensities.reshape(modes, quarter, width),
    )
    terms, mixed = local(
        functools.partial(inverse_kernel, tiles),
        [SMEM] + [VMEM] * 8,
        [shape(tiles, rounds, block, 2 * width), shape(width, 3 * width)],
    )(place_now, ratio.reshape(width, width), far, window, probe, *tables)
    everything, probe_next = remote(
        functools.partial(reduce_kernel, sizes),
        2,
        3,
        [shape(count, rounds, block, 2 * width), shape(count, share, 2 * width)],
        [
            pltpu.VMEM((modes, rounds, block, 2 * width), f32),
            pltpu.VMEM((count, share, 3 * width), f32),
            pltpu.VMEM((rounds, block, 2 * width), f32),
        ]
        + [dma(modes - 1)] * 2
        + [dma(count - 1)] * 2
        + [dma(scans * modes), dma(count)]
        + [dma(count - 1)] * 2,
    )(
        terms,
        mixed.reshape(count, share, 3 * width),
        probe.reshape(count, share, 2 * width),
    )
    own = jnp.stack([tile, tile])[None].astype(jnp.int32)
    updated = local(
        functools.partial(update_kernel, tiles),
        [SMEM] + [VMEM] * 3,
        shape(cycles, 2, block, columns),
        [pltpu.VMEM((cycles, block, columns), f32)],
    )(
        jnp.concatenate([places, own], 0),
        everything,
        squares.reshape(blocks, block, width),
        planar,
    )
    new_object = jnp.swapaxes(updated, 1, 2)[:, None]
    return (new_object, probe_next.reshape(1, width, 2 * width))


def solution(mesh):
    in_specs = (
        P(None, "tile", None, None, None),
        P("mode", None, None),
        P(("scan", "tile"), None, None),
        P(),
    )
    out_specs = (P(None, "tile", None, None, None), P("mode", None, None))
    sizes = (mesh.shape["scan"], mesh.shape["tile"], mesh.shape["mode"])

    def run(object_field, probe_modes, intensities, positions):
        body = on_device
        if (
            sizes[1] == sizes[2]
            and probe_modes.shape[0] == sizes[2]
            and intensities.shape[0] == sizes[0] * sizes[1]
        ):
            tables = [jnp.asarray(table) for table in split_tables(probe_modes.shape[1])]
            body = functools.partial(one_wave, sizes, tables)
        return jax.shard_map(
            body, mesh=mesh, in_specs=in_specs, out_specs=out_specs, check_vma=False
        )(object_field, probe_modes, intensities, positions)

    return run
```

```python
import functools
import math

import jax
import jax.numpy as jnp
import ml_dtypes
import numpy as np
from jax import lax
from jax.experimental import pallas as pl
from jax.experimental.pallas import tpu as pltpu
from jax.sharding import PartitionSpec as P

floor_level = 0.1
damping = 1.0
highest = lax.Precision.HIGHEST


def transform_tables(width):
    index = jnp.arange(width, dtype=jnp.int32)
    phase = (index[:, None] * index[None, :] % width).astype(jnp.float32)
    angle = phase * (2.0 * math.pi / width)
    cosine = jnp.cos(angle) / math.sqrt(width)
    sine = -jnp.sin(angle) / math.sqrt(width)
    forward_rows = jnp.block([[cosine, sine], [-sine, cosine]])
    inverse_rows = jnp.block([[cosine, -sine], [sine, cosine]])
    return (cosine, sine, forward_rows, inverse_rows)


def times(left, right):
    half = left.shape[-1] // 2
    return jnp.concatenate(
        [
            left[..., :half] * right[..., :half] - left[..., half:] * right[..., half:],
            left[..., :half] * right[..., half:] + left[..., half:] * right[..., :half],
        ],
        -1,
    )


def conj_times(left, right):
    half = left.shape[-1] // 2
    return jnp.concatenate(
        [
            left[..., :half] * right[..., :half] + left[..., half:] * right[..., half:],
            left[..., :half] * right[..., half:] - left[..., half:] * right[..., :half],
        ],
        -1,
    )


def power(values):
    half = values.shape[-1] // 2
    return values[..., :half] ** 2 + values[..., half:] ** 2


def columns_forward(cosine, sine, data):
    half = data.shape[-1] // 2
    first = jnp.einsum("ab,pbc->pac", cosine, data, precision=highest)
    second = jnp.einsum("ab,pbc->pac", sine, data, precision=highest)
    return jnp.concatenate(
        [first[..., :half] - second[..., half:], first[..., half:] + second[..., :half]], -1
    )


def columns_inverse(cosine, sine, data):
    half = data.shape[-1] // 2
    first = jnp.einsum("ab,pbc->pac", cosine, data, precision=highest)
    second = jnp.einsum("ab,pbc->pac", sine, data, precision=highest)
    return jnp.concatenate(
        [first[..., :half] + second[..., half:], first[..., half:] - second[..., :half]], -1
    )


def project(cosine, sine, spectra, intensities):
    far_field = columns_forward(cosine, sine, spectra)
    total_power = lax.psum(power(far_field), "mode")
    ratio_map = jnp.sqrt(intensities / jnp.maximum(total_power, floor_level))
    return columns_inverse(cosine, sine, far_field * jnp.concatenate([ratio_map, ratio_map], -1))


def pick_rows(rows, picks):
    return rows[picks]


def assemble(received, order):
    moved = jnp.swapaxes(received, 0, 1)
    picked = jax.vmap(pick_rows)(moved, order)
    ordered = jnp.swapaxes(picked, 1, 2)
    return ordered.reshape(ordered.shape[0], -1, ordered.shape[-1])


def disassemble(ordered, order):
    moved = jnp.swapaxes(ordered, 1, 2)
    picked = jax.vmap(pick_rows)(moved, order)
    return jnp.swapaxes(picked, 0, 1)


def place(cycle_flat, col_flat, terms, weights, shape):
    cycle_count, block, columns = shape
    count, rows, doubled = terms.shape
    width = doubled // 2
    span = jnp.arange(width, dtype=jnp.int32)
    split_terms = terms.reshape(count, rows, 2, width)
    numerator = jnp.zeros((cycle_count, block, 2, columns), jnp.float32)
    numerator = numerator.at[
        cycle_flat[:, None, None, None],
        jnp.arange(rows, dtype=jnp.int32)[None, :, None, None],
        jnp.arange(2, dtype=jnp.int32)[None, None, :, None],
        col_flat[:, None, None, None] + span,
    ].add(split_terms)
    weight = jnp.zeros((cycle_count, block, columns), jnp.float32)
    weight = weight.at[
        cycle_flat[:, None, None],
        jnp.arange(block, dtype=jnp.int32)[None, :, None],
        col_flat[:, None, None] + span,
    ].add(weights)
    return (numerator, weight)


def on_device(object_field, probe_modes, intensities, positions):
    width = probe_modes.shape[1]
    cycles = object_field.shape[0]
    block = object_field.shape[2]
    columns = object_field.shape[4]
    tiles = lax.axis_size("tile")
    patterns = intensities.shape[0]
    blocks = width // block
    rounds = blocks // tiles
    scan_index = lax.axis_index("scan")
    tile_index = lax.axis_index("tile")
    group = lax.dynamic_slice_in_dim(
        positions, scan_index * (tiles * patterns), tiles * patterns, 0
    )
    group = group.reshape(tiles, patterns, 2)
    start_blocks = group[:, :, 0] // block
    start_cols = group[:, :, 1]
    own_starts = lax.dynamic_index_in_dim(start_blocks, tile_index, 0, keepdims=False)
    first_block = jnp.mod(tile_index - start_blocks, tiles)
    patch_blocks = first_block[:, :, None] + tiles * jnp.arange(rounds, dtype=jnp.int32)
    cycle_flat = ((start_blocks[:, :, None] + patch_blocks) // tiles).reshape(-1)
    col_flat = jnp.broadcast_to(start_cols[:, :, None], patch_blocks.shape).reshape(-1)
    patch_flat = patch_blocks.reshape(-1)
    count = patch_flat.shape[0]
    lanes = jnp.arange(tiles, dtype=jnp.int32)
    gather_order = jnp.mod(lanes[None, :] + own_starts[:, None], tiles)
    scatter_order = jnp.mod(lanes[None, :] - own_starts[:, None], tiles)
    cosine, sine, forward_rows, inverse_rows = transform_tables(width)
    selector = (patch_flat[None, :] == jnp.arange(blocks, dtype=jnp.int32)[:, None]).astype(
        jnp.float32
    )
    current = object_field[:, 0]
    probe_now = probe_modes[0]

    def cut(cycle, column):
        piece = lax.dynamic_slice(current, (cycle, 0, 0, column), (1, block, 2, width))
        return piece.reshape(block, 2 * width)

    object_rows = jax.vmap(cut)(cycle_flat, col_flat)
    probe_rows = probe_now.reshape(blocks, block, 2 * width)[patch_flat]
    exit_rows = times(probe_rows, object_rows)
    spectra = jnp.dot(exit_rows.reshape(-1, 2 * width), forward_rows, precision=highest)
    arrived = lax.all_to_all(
        spectra.reshape(tiles, patterns, rounds, block, 2 * width),
        "tile",
        split_axis=0,
        concat_axis=0,
        tiled=True,
    )
    returned = project(cosine, sine, assemble(arrived, gather_order), intensities)
    outgoing = disassemble(
        returned.reshape(patterns, rounds, tiles, block, 2 * width), scatter_order
    )
    came_back = lax.all_to_all(outgoing, "tile", split_axis=0, concat_axis=0, tiled=True)
    new_rows = jnp.dot(came_back.reshape(-1, 2 * width), inverse_rows, precision=highest)
    difference = new_rows.reshape(count, block, 2 * width) - exit_rows
    terms = conj_times(probe_rows, difference)
    mixed = jnp.concatenate([conj_times(object_rows, difference), power(object_rows)], -1)
    probe_stats = jnp.dot(selector, mixed.reshape(count, -1), precision=highest).reshape(
        width, 3 * width
    )
    numerator, weight = place(
        cycle_flat, col_flat, terms, power(probe_rows), (cycles, block, columns)
    )
    numerator, weight = lax.psum((numerator, weight), ("scan", "mode"))
    summed = lax.psum(probe_stats, ("scan", "tile"))
    divisor = summed[:, 2 * width :]
    probe_next = probe_now + summed[:, : 2 * width] / jnp.concatenate([divisor, divisor], -1)
    current = current + numerator / (weight[:, :, None, :] + damping)
    return (current[:, None], probe_next[None])


MESH = pl.DeviceIdType.MESH
VMEM = pl.BlockSpec(memory_space=pltpu.VMEM)
SMEM = pl.BlockSpec(memory_space=pltpu.SMEM)
vmem_bytes = 40 * 1024 * 1024
f32 = jnp.float32


def split_tables(width):
    index = np.arange(width)
    angle = (index[:, None] * index[None, :] % width) * (2.0 * math.pi / width)
    cosine = np.cos(angle) / math.sqrt(width)
    sine = -np.sin(angle) / math.sqrt(width)
    right = np.block([[cosine, sine], [-sine, cosine]])
    parts = []
    for table in (right, right.T):
        high = table.astype(ml_dtypes.bfloat16)
        low = (table - high.astype(np.float64)).astype(ml_dtypes.bfloat16)
        parts += [high, low]
    return parts


def halves(values):
    high = values.astype(jnp.bfloat16)
    return high, (values - high.astype(f32)).astype(jnp.bfloat16)


def dot(left, right):
    return jnp.dot(left, right, preferred_element_type=f32)


def right_product(values, high_table, low_table):
    high, low = halves(values)
    return dot(high, high_table) + (dot(low, high_table) + dot(high, low_table))


def left_product(high_table, low_table, values):
    half = values.shape[-1] // 2
    high, low = halves(jnp.concatenate([values[:, :half], values[:, half:]], 0))
    out = dot(high_table, high) + (dot(high_table, low) + dot(low_table, high))
    rows = out.shape[0] // 2
    return jnp.concatenate([out[:rows], out[rows:]], 1)


def sends(me, count, id_of, src_of, dst, send, recv):
    copies = []
    for step in range(1, count):
        peer = lax.rem(me + step, count)
        copies.append(
            pltpu.make_async_remote_copy(
                src_ref=src_of(peer),
                dst_ref=dst.at[me],
                send_sem=send.at[step - 1],
                recv_sem=recv.at[step - 1],
                device_id=id_of(peer),
                device_id_type=MESH,
            )
        )
    for copy in copies:
        copy.start()
    return copies


def greet(groups):
    barrier = pltpu.get_barrier_semaphore()
    total = 0
    for me, count, id_of in groups:
        for step in range(1, count):
            pl.semaphore_signal(
                barrier, inc=1, device_id=id_of(lax.rem(me + step, count)), device_id_type=MESH
            )
            total += 1
    pl.semaphore_wait(barrier, total)


def tile_id(peer):
    return {"tile": peer}


def mode_id(peer):
    return {"mode": peer}


def pattern_id(tiles, peer):
    return {"scan": peer // tiles, "tile": lax.rem(peer, tiles)}


def round_id(scans, peer):
    return {"scan": lax.rem(peer, scans), "mode": peer // scans}


def place_of(places_ref, index, block):
    return places_ref[0, index] // block, places_ref[1, index]


def fetch_kernel(
    sizes, places_ref, object_ref, probe_ref, got_ref, squares_ref,
    rows, square, send, recv, send_p, recv_p,
):
    scans, tiles, modes = sizes
    scan, tile, mode = lax.axis_index("scan"), lax.axis_index("tile"), lax.axis_index("mode")
    block = object_ref.shape[2]
    rounds = rows.shape[1]
    for index in range(tiles):
        start, _ = place_of(places_ref, scan * tiles + index, block)
        first = (start + lax.rem(tile - start + tiles * block * block, tiles)) // tiles
        rows[index] = object_ref[pl.ds(first, rounds)]
    share = square.shape[0]
    square[...] = power(probe_ref[pl.ds((scan * tiles + tile) * share, share)])
    greet([(tile, tiles, tile_id), (mode, modes, mode_id)])
    copies = sends(tile, tiles, tile_id, lambda peer: rows.at[peer], got_ref, send, recv)
    copies += sends(mode, modes, mode_id, lambda peer: square, squares_ref, send_p, recv_p)
    got_ref[tile] = rows[tile]
    squares_ref[mode] = square[...]
    for copy in copies:
        copy.wait()


def forward_kernel(
    sizes, places_ref, got_ref, squares_ref, probe_ref, rh, rl, gh, gl,
    window_ref, far_ref, power_ref, square_ref,
):
    width = probe_ref.shape[0]
    block = got_ref.shape[3]
    columns = got_ref.shape[4]
    tiles = sizes[1]
    me = lax.axis_index("scan") * tiles + lax.axis_index("tile")
    start, col = place_of(places_ref, me, block)
    shift = lax.rem(columns - col, columns)
    for index in range(width // block):
        owner = lax.rem(start + index, tiles)
        for part in range(2):
            piece = got_ref[owner, index // tiles, part]
            window_ref[index * block : (index + 1) * block, part * width : (part + 1) * width] = (
                pltpu.roll(piece, shift, 1)[:, :width]
            )
    waves = times(probe_ref[...], window_ref[...])
    far = left_product(gh[...], gl[...], right_product(waves, rh[...], rl[...]))
    far_ref[...] = far
    power_ref[...] = power(far)
    square_ref[...] = jnp.sum(squares_ref[...], axis=0)


def ratio_kernel(
    sizes, power_ref, square_ref, measured_ref, ratio_ref, squares_ref,
    got, send, recv, send_r, recv_r, send_p, recv_p,
):
    scans, tiles, modes = sizes
    mode = lax.axis_index("mode")
    me = lax.axis_index("scan") * tiles + lax.axis_index("tile")
    id_of = functools.partial(pattern_id, tiles)
    greet([(mode, modes, mode_id), (me, scans * tiles, id_of)])
    first = sends(mode, modes, mode_id, lambda peer: power_ref.at[peer], got, send, recv)
    other = sends(me, scans * tiles, id_of, lambda peer: square_ref, squares_ref, send_p, recv_p)
    got[mode] = power_ref[mode]
    squares_ref[me] = square_ref[...]
    for copy in first:
        copy.wait()
    total = got[0]
    for index in range(1, modes):
        total = total + got[index]
    ratio_ref[mode] = jnp.sqrt(measured_ref[mode] / jnp.maximum(total, floor_level))
    last = sends(
        mode, modes, mode_id, lambda peer: ratio_ref.at[mode], ratio_ref, send_r, recv_r
    )
    for copy in last + other:
        copy.wait()


def inverse_kernel(
    sizes, places_ref, ratio_ref, far_ref, window_ref, probe_ref, rh, rl, gh, gl,
    terms_ref, mixed_ref,
):
    width = probe_ref.shape[0]
    block = terms_ref.shape[2]
    tiles = sizes[1]
    count = sizes[0] * tiles
    me = lax.axis_index("scan") * tiles + lax.axis_index("tile")
    start, _ = place_of(places_ref, me, block)
    ratio = ratio_ref[...]
    scaled = far_ref[...] * jnp.concatenate([ratio, ratio], 1)
    waves = left_product(rh[...], rl[...], right_product(scaled, gh[...], gl[...]))
    probe, window = probe_ref[...], window_ref[...]
    difference = waves - times(probe, window)
    terms = conj_times(probe, difference)
    for index in range(width // block):
        owner = lax.rem(start + index, count)
        terms_ref[owner, index // count] = terms[index * block : (index + 1) * block]
    mixed_ref[...] = jnp.concatenate([conj_times(window, difference), power(window)], 1)


def reduce_kernel(
    sizes, places_ref, terms_ref, mixed_ref, probe_ref, square_ref, object_ref,
    out_ref, next_ref,
    got_t, got_p, canvas, got_c,
    send_t, recv_t, send_m, recv_m, send_c, recv_c, send_o, recv_o, send_n, recv_n,
):
    scans, tiles, modes = sizes
    count = scans * tiles
    rounds, block, width2 = terms_ref.shape[1:]
    width = width2 // 2
    columns = object_ref.shape[-1]
    scan, tile, mode = lax.axis_index("scan"), lax.axis_index("tile"), lax.axis_index("mode")
    me = scan * tiles + tile
    cycle = scan + scans * mode
    id_of = functools.partial(pattern_id, tiles)
    id_round = functools.partial(round_id, scans)
    greet([(me, count, id_of), (cycle, scans * modes, id_round)])
    moves_t = sends(me, count, id_of, lambda peer: terms_ref.at[peer], got_t, send_t, recv_t)
    moves_p = sends(me, count, id_of, lambda peer: mixed_ref.at[peer], got_p, send_m, recv_m)
    got_t[me] = terms_ref[me]
    got_p[me] = mixed_ref[me]
    blank = jnp.zeros((block, columns - width), f32)
    zero = jnp.zeros((block, columns), f32)

    def spread(piece, col):
        return pltpu.roll(jnp.concatenate([piece, blank], 1), col, 1)

    weight = zero
    for index in range(count):
        start, col = place_of(places_ref, index, block)
        which = me + count * mode - start
        inside = jnp.logical_and(which >= 0, which < count * rounds)
        piece = square_ref[jnp.clip(which, 0, count * rounds - 1)]
        weight = weight + jnp.where(inside, spread(piece, col), 0.0)
    for copy in moves_t:
        copy.wait()
    for part in range(2):
        sums = [zero] * modes
        for index in range(count):
            start, col = place_of(places_ref, index, block)
            first = (start + lax.rem(me - start + count * block * block, count)) // count
            for step in range(rounds):
                piece = spread(got_t[index, step, :, part * width : (part + 1) * width], col)
                for slot in range(modes):
                    sums[slot] = sums[slot] + jnp.where(first + step == slot, piece, 0.0)
        for slot in range(modes):
            canvas[slot, part] = sums[slot]
    moves_c = sends(mode, modes, mode_id, lambda peer: canvas.at[peer], got_c, send_c, recv_c)
    got_c[mode] = canvas[mode]
    for copy in moves_c:
        copy.wait()
    for part in range(2):
        total = got_c[0, part]
        for index in range(1, modes):
            total = total + got_c[index, part]
        out_ref[cycle, part] = object_ref[cycle, part] + total / (weight + damping)
    last = sends(
        cycle, scans * modes, id_round, lambda peer: out_ref.at[cycle], out_ref, send_o, recv_o
    )
    for copy in moves_p:
        copy.wait()
    totals = got_p[0]
    for index in range(1, count):
        totals = totals + got_p[index]
    divisor = totals[:, width2:]
    next_ref[me] = probe_ref[me] + totals[:, :width2] / jnp.concatenate([divisor, divisor], 1)
    last += sends(me, count, id_of, lambda peer: next_ref.at[me], next_ref, send_n, recv_n)
    for copy in last:
        copy.wait()


def shape(*dims):
    return jax.ShapeDtypeStruct(dims, f32)


def dma(count):
    return pltpu.SemaphoreType.DMA((count,))


def local(kernel, in_specs, outs, scratch=()):
    return pl.pallas_call(
        kernel,
        out_shape=outs,
        in_specs=in_specs,
        out_specs=jax.tree.map(lambda _: VMEM, outs),
        scratch_shapes=list(scratch),
        compiler_params=pltpu.CompilerParams(vmem_limit_bytes=vmem_bytes),
    )


def remote(kernel, number, inputs, outs, scratch):
    return pl.pallas_call(
        kernel,
        out_shape=outs,
        in_specs=inputs,
        out_specs=[VMEM] * len(outs),
        scratch_shapes=scratch,
        compiler_params=pltpu.CompilerParams(
            collective_id=number, has_side_effects=True, vmem_limit_bytes=vmem_bytes
        ),
    )


def one_wave(sizes, tables, object_field, probe_modes, intensities, positions):
    scans, tiles, modes = sizes
    count = scans * tiles
    width = probe_modes.shape[1]
    cycles, _, block, _, columns = object_field.shape
    blocks = width // block
    rounds = blocks // tiles
    share = width // count
    quarter = width // modes
    places = positions.T
    probe = probe_modes[0]
    planar = jnp.swapaxes(object_field[:, 0], 1, 2)
    got, squares = remote(
        functools.partial(fetch_kernel, sizes),
        0,
        [SMEM, VMEM, VMEM],
        [shape(tiles, rounds, 2, block, columns), shape(modes, share, width)],
        [
            pltpu.VMEM((tiles, rounds, 2, block, columns), f32),
            pltpu.VMEM((share, width), f32),
        ]
        + [dma(tiles - 1)] * 2
        + [dma(modes - 1)] * 2,
    )(places, planar, probe)
    window, far, strength, square = local(
        functools.partial(forward_kernel, sizes),
        [SMEM] + [VMEM] * 7,
        [
            shape(width, 2 * width),
            shape(width, 2 * width),
            shape(width, width),
            shape(share, width),
        ],
    )(places, got, squares, probe, *tables)
    ratio, squares = remote(
        functools.partial(ratio_kernel, sizes),
        1,
        [VMEM] * 3,
        [shape(modes, quarter, width), shape(count, share, width)],
        [pltpu.VMEM((modes, quarter, width), f32)]
        + [dma(modes - 1)] * 4
        + [dma(count - 1)] * 2,
    )(
        strength.reshape(modes, quarter, width),
        square,
        intensities.reshape(modes, quarter, width),
    )
    parts = blocks // count
    terms, mixed = local(
        functools.partial(inverse_kernel, sizes),
        [SMEM] + [VMEM] * 8,
        [shape(count, parts, block, 2 * width), shape(width, 3 * width)],
    )(places, ratio.reshape(width, width), far, window, probe, *tables)
    updated, probe_next = remote(
        functools.partial(reduce_kernel, sizes),
        2,
        [SMEM] + [VMEM] * 5,
        [shape(cycles, 2, block, columns), shape(count, share, 2 * width)],
        [
            pltpu.VMEM((count, parts, block, 2 * width), f32),
            pltpu.VMEM((count, share, 3 * width), f32),
            pltpu.VMEM((modes, 2, block, columns), f32),
            pltpu.VMEM((modes, 2, block, columns), f32),
        ]
        + [dma(count - 1)] * 4
        + [dma(modes - 1)] * 2
        + [dma(cycles - 1)] * 2
        + [dma(count - 1)] * 2,
    )(
        places,
        terms,
        mixed.reshape(count, share, 3 * width),
        probe.reshape(count, share, 2 * width),
        squares.reshape(blocks, block, width),
        planar,
    )
    new_object = jnp.swapaxes(updated, 1, 2)[:, None]
    return (new_object, probe_next.reshape(1, width, 2 * width))


def solution(mesh):
    in_specs = (
        P(None, "tile", None, None, None),
        P("mode", None, None),
        P(("scan", "tile"), None, None),
        P(),
    )
    out_specs = (P(None, "tile", None, None, None), P("mode", None, None))
    sizes = (mesh.shape["scan"], mesh.shape["tile"], mesh.shape["mode"])

    def run(object_field, probe_modes, intensities, positions):
        body = on_device
        if (
            object_field.shape[0] == sizes[0] * sizes[2]
            and probe_modes.shape[0] == sizes[2]
            and intensities.shape[0] == sizes[0] * sizes[1]
            and probe_modes.shape[1] % (object_field.shape[2] * sizes[0] * sizes[1]) == 0
        ):
            tables = [jnp.asarray(table) for table in split_tables(probe_modes.shape[1])]
            body = functools.partial(one_wave, sizes, tables)
        return jax.shard_map(
            body, mesh=mesh, in_specs=in_specs, out_specs=out_specs, check_vma=False
        )(object_field, probe_modes, intensities, positions)

    return run
```

```python
import functools
import math

import jax
import jax.numpy as jnp
import ml_dtypes
import numpy as np
from jax import lax
from jax.experimental import pallas as pl
from jax.experimental.pallas import tpu as pltpu
from jax.sharding import PartitionSpec as P

floor_level = 0.1
damping = 1.0
highest = lax.Precision.HIGHEST


def transform_tables(width):
    index = jnp.arange(width, dtype=jnp.int32)
    phase = (index[:, None] * index[None, :] % width).astype(jnp.float32)
    angle = phase * (2.0 * math.pi / width)
    cosine = jnp.cos(angle) / math.sqrt(width)
    sine = -jnp.sin(angle) / math.sqrt(width)
    forward_rows = jnp.block([[cosine, sine], [-sine, cosine]])
    inverse_rows = jnp.block([[cosine, -sine], [sine, cosine]])
    return (cosine, sine, forward_rows, inverse_rows)


def times(left, right):
    half = left.shape[-1] // 2
    return jnp.concatenate(
        [
            left[..., :half] * right[..., :half] - left[..., half:] * right[..., half:],
            left[..., :half] * right[..., half:] + left[..., half:] * right[..., :half],
        ],
        -1,
    )


def conj_times(left, right):
    half = left.shape[-1] // 2
    return jnp.concatenate(
        [
            left[..., :half] * right[..., :half] + left[..., half:] * right[..., half:],
            left[..., :half] * right[..., half:] - left[..., half:] * right[..., :half],
        ],
        -1,
    )


def power(values):
    half = values.shape[-1] // 2
    return values[..., :half] ** 2 + values[..., half:] ** 2


def columns_forward(cosine, sine, data):
    half = data.shape[-1] // 2
    first = jnp.einsum("ab,pbc->pac", cosine, data, precision=highest)
    second = jnp.einsum("ab,pbc->pac", sine, data, precision=highest)
    return jnp.concatenate(
        [first[..., :half] - second[..., half:], first[..., half:] + second[..., :half]], -1
    )


def columns_inverse(cosine, sine, data):
    half = data.shape[-1] // 2
    first = jnp.einsum("ab,pbc->pac", cosine, data, precision=highest)
    second = jnp.einsum("ab,pbc->pac", sine, data, precision=highest)
    return jnp.concatenate(
        [first[..., :half] + second[..., half:], first[..., half:] - second[..., :half]], -1
    )


def project(cosine, sine, spectra, intensities):
    far_field = columns_forward(cosine, sine, spectra)
    total_power = lax.psum(power(far_field), "mode")
    ratio_map = jnp.sqrt(intensities / jnp.maximum(total_power, floor_level))
    return columns_inverse(cosine, sine, far_field * jnp.concatenate([ratio_map, ratio_map], -1))


def pick_rows(rows, picks):
    return rows[picks]


def assemble(received, order):
    moved = jnp.swapaxes(received, 0, 1)
    picked = jax.vmap(pick_rows)(moved, order)
    ordered = jnp.swapaxes(picked, 1, 2)
    return ordered.reshape(ordered.shape[0], -1, ordered.shape[-1])


def disassemble(ordered, order):
    moved = jnp.swapaxes(ordered, 1, 2)
    picked = jax.vmap(pick_rows)(moved, order)
    return jnp.swapaxes(picked, 0, 1)


def place(cycle_flat, col_flat, terms, weights, shape):
    cycle_count, block, columns = shape
    count, rows, doubled = terms.shape
    width = doubled // 2
    span = jnp.arange(width, dtype=jnp.int32)
    split_terms = terms.reshape(count, rows, 2, width)
    numerator = jnp.zeros((cycle_count, block, 2, columns), jnp.float32)
    numerator = numerator.at[
        cycle_flat[:, None, None, None],
        jnp.arange(rows, dtype=jnp.int32)[None, :, None, None],
        jnp.arange(2, dtype=jnp.int32)[None, None, :, None],
        col_flat[:, None, None, None] + span,
    ].add(split_terms)
    weight = jnp.zeros((cycle_count, block, columns), jnp.float32)
    weight = weight.at[
        cycle_flat[:, None, None],
        jnp.arange(block, dtype=jnp.int32)[None, :, None],
        col_flat[:, None, None] + span,
    ].add(weights)
    return (numerator, weight)


def on_device(object_field, probe_modes, intensities, positions):
    width = probe_modes.shape[1]
    cycles = object_field.shape[0]
    block = object_field.shape[2]
    columns = object_field.shape[4]
    tiles = lax.axis_size("tile")
    patterns = intensities.shape[0]
    blocks = width // block
    rounds = blocks // tiles
    scan_index = lax.axis_index("scan")
    tile_index = lax.axis_index("tile")
    group = lax.dynamic_slice_in_dim(
        positions, scan_index * (tiles * patterns), tiles * patterns, 0
    )
    group = group.reshape(tiles, patterns, 2)
    start_blocks = group[:, :, 0] // block
    start_cols = group[:, :, 1]
    own_starts = lax.dynamic_index_in_dim(start_blocks, tile_index, 0, keepdims=False)
    first_block = jnp.mod(tile_index - start_blocks, tiles)
    patch_blocks = first_block[:, :, None] + tiles * jnp.arange(rounds, dtype=jnp.int32)
    cycle_flat = ((start_blocks[:, :, None] + patch_blocks) // tiles).reshape(-1)
    col_flat = jnp.broadcast_to(start_cols[:, :, None], patch_blocks.shape).reshape(-1)
    patch_flat = patch_blocks.reshape(-1)
    count = patch_flat.shape[0]
    lanes = jnp.arange(tiles, dtype=jnp.int32)
    gather_order = jnp.mod(lanes[None, :] + own_starts[:, None], tiles)
    scatter_order = jnp.mod(lanes[None, :] - own_starts[:, None], tiles)
    cosine, sine, forward_rows, inverse_rows = transform_tables(width)
    selector = (patch_flat[None, :] == jnp.arange(blocks, dtype=jnp.int32)[:, None]).astype(
        jnp.float32
    )
    current = object_field[:, 0]
    probe_now = probe_modes[0]

    def cut(cycle, column):
        piece = lax.dynamic_slice(current, (cycle, 0, 0, column), (1, block, 2, width))
        return piece.reshape(block, 2 * width)

    object_rows = jax.vmap(cut)(cycle_flat, col_flat)
    probe_rows = probe_now.reshape(blocks, block, 2 * width)[patch_flat]
    exit_rows = times(probe_rows, object_rows)
    spectra = jnp.dot(exit_rows.reshape(-1, 2 * width), forward_rows, precision=highest)
    arrived = lax.all_to_all(
        spectra.reshape(tiles, patterns, rounds, block, 2 * width),
        "tile",
        split_axis=0,
        concat_axis=0,
        tiled=True,
    )
    returned = project(cosine, sine, assemble(arrived, gather_order), intensities)
    outgoing = disassemble(
        returned.reshape(patterns, rounds, tiles, block, 2 * width), scatter_order
    )
    came_back = lax.all_to_all(outgoing, "tile", split_axis=0, concat_axis=0, tiled=True)
    new_rows = jnp.dot(came_back.reshape(-1, 2 * width), inverse_rows, precision=highest)
    difference = new_rows.reshape(count, block, 2 * width) - exit_rows
    terms = conj_times(probe_rows, difference)
    mixed = jnp.concatenate([conj_times(object_rows, difference), power(object_rows)], -1)
    probe_stats = jnp.dot(selector, mixed.reshape(count, -1), precision=highest).reshape(
        width, 3 * width
    )
    numerator, weight = place(
        cycle_flat, col_flat, terms, power(probe_rows), (cycles, block, columns)
    )
    numerator, weight = lax.psum((numerator, weight), ("scan", "mode"))
    summed = lax.psum(probe_stats, ("scan", "tile"))
    divisor = summed[:, 2 * width :]
    probe_next = probe_now + summed[:, : 2 * width] / jnp.concatenate([divisor, divisor], -1)
    current = current + numerator / (weight[:, :, None, :] + damping)
    return (current[:, None], probe_next[None])


MESH = pl.DeviceIdType.MESH
VMEM = pl.BlockSpec(memory_space=pltpu.VMEM)
SMEM = pl.BlockSpec(memory_space=pltpu.SMEM)
vmem_bytes = 40 * 1024 * 1024
f32 = jnp.float32


def split_tables(width):
    index = np.arange(width)
    angle = (index[:, None] * index[None, :] % width) * (2.0 * math.pi / width)
    cosine = np.cos(angle) / math.sqrt(width)
    sine = -np.sin(angle) / math.sqrt(width)
    right = np.block([[cosine, sine], [-sine, cosine]])
    parts = []
    for table in (right, right.T):
        high = table.astype(ml_dtypes.bfloat16)
        low = (table - high.astype(np.float64)).astype(ml_dtypes.bfloat16)
        parts += [high, low]
    return parts


def halves(values):
    high = values.astype(jnp.bfloat16)
    return high, (values - high.astype(f32)).astype(jnp.bfloat16)


def dot(left, right):
    return jnp.dot(left, right, preferred_element_type=f32)


def right_product(values, high_table, low_table):
    high, low = halves(values)
    return dot(high, high_table) + (dot(low, high_table) + dot(high, low_table))


def left_product(high_table, low_table, values):
    half = values.shape[-1] // 2
    high, low = halves(jnp.concatenate([values[:, :half], values[:, half:]], 0))
    out = dot(high_table, high) + (dot(high_table, low) + dot(low_table, high))
    rows = out.shape[0] // 2
    return jnp.concatenate([out[:rows], out[rows:]], 1)


def sends(me, count, id_of, src_of, dst, send, recv):
    copies = []
    for step in range(1, count):
        peer = lax.rem(me + step, count)
        copies.append(
            pltpu.make_async_remote_copy(
                src_ref=src_of(peer),
                dst_ref=dst.at[me],
                send_sem=send.at[step - 1],
                recv_sem=recv.at[step - 1],
                device_id=id_of(peer),
                device_id_type=MESH,
            )
        )
    for copy in copies:
        copy.start()
    return copies


def greet(groups):
    barrier = pltpu.get_barrier_semaphore()
    total = 0
    for me, count, id_of in groups:
        for step in range(1, count):
            pl.semaphore_signal(
                barrier, inc=1, device_id=id_of(lax.rem(me + step, count)), device_id_type=MESH
            )
            total += 1
    pl.semaphore_wait(barrier, total)


def tile_id(peer):
    return {"tile": peer}


def mode_id(peer):
    return {"mode": peer}


def pattern_id(tiles, peer):
    return {"scan": peer // tiles, "tile": lax.rem(peer, tiles)}


def round_id(scans, peer):
    return {"scan": lax.rem(peer, scans), "mode": peer // scans}


def place_of(places_ref, index, block):
    return places_ref[0, index] // block, places_ref[1, index]


def fetch_kernel(
    sizes, places_ref, object_ref, probe_ref, got_ref, squares_ref,
    rows, square, send, recv, send_p, recv_p,
):
    scans, tiles, modes = sizes
    scan, tile, mode = lax.axis_index("scan"), lax.axis_index("tile"), lax.axis_index("mode")
    block = object_ref.shape[2]
    columns = object_ref.shape[3]
    rounds, width = rows.shape[1], rows.shape[4]
    for index in range(tiles):
        start, col = place_of(places_ref, scan * tiles + index, block)
        first = (start + lax.rem(tile - start + tiles * block * block, tiles)) // tiles
        piece = object_ref[pl.ds(first, rounds)].reshape(rounds * 2 * block, columns)
        piece = pltpu.roll(piece, lax.rem(columns - col, columns), 1)[:, :width]
        rows[index] = piece.reshape(rounds, 2, block, width)
    share = square.shape[0]
    square[...] = power(probe_ref[pl.ds((scan * tiles + tile) * share, share)])
    greet([(tile, tiles, tile_id), (mode, modes, mode_id)])
    copies = sends(tile, tiles, tile_id, lambda peer: rows.at[peer], got_ref, send, recv)
    copies += sends(mode, modes, mode_id, lambda peer: square, squares_ref, send_p, recv_p)
    got_ref[tile] = rows[tile]
    squares_ref[mode] = square[...]
    for copy in copies:
        copy.wait()


def forward_kernel(
    sizes, places_ref, got_ref, squares_ref, probe_ref, rh, rl, gh, gl,
    window_ref, far_ref, power_ref, square_ref, bright_ref,
):
    width = probe_ref.shape[0]
    block = got_ref.shape[3]
    tiles = sizes[1]
    me = lax.axis_index("scan") * tiles + lax.axis_index("tile")
    start, _ = place_of(places_ref, me, block)
    for index in range(width // block):
        owner = lax.rem(start + index, tiles)
        for part in range(2):
            window_ref[index * block : (index + 1) * block, part * width : (part + 1) * width] = (
                got_ref[owner, index // tiles, part]
            )
    waves = times(probe_ref[...], window_ref[...])
    far = left_product(gh[...], gl[...], right_product(waves, rh[...], rl[...]))
    far_ref[...] = far
    power_ref[...] = power(far)
    square_ref[...] = jnp.sum(squares_ref[...], axis=0)
    bright_ref[...] = power(window_ref[...])


def ratio_kernel(
    sizes, power_ref, square_ref, bright_ref, measured_ref, ratio_ref, squares_ref, sum_ref,
    got, got_b, send, recv, send_r, recv_r, send_p, recv_p, send_b, recv_b,
):
    scans, tiles, modes = sizes
    mode = lax.axis_index("mode")
    me = lax.axis_index("scan") * tiles + lax.axis_index("tile")
    id_of = functools.partial(pattern_id, tiles)
    greet([(mode, modes, mode_id), (me, scans * tiles, id_of)])
    first = sends(mode, modes, mode_id, lambda peer: power_ref.at[peer], got, send, recv)
    other = sends(me, scans * tiles, id_of, lambda peer: square_ref, squares_ref, send_p, recv_p)
    more = sends(
        me, scans * tiles, id_of, lambda peer: bright_ref.at[peer], got_b, send_b, recv_b
    )
    got_b[me] = bright_ref[me]
    got[mode] = power_ref[mode]
    squares_ref[me] = square_ref[...]
    for copy in first:
        copy.wait()
    total = got[0]
    for index in range(1, modes):
        total = total + got[index]
    ratio_ref[mode] = jnp.sqrt(measured_ref[mode] / jnp.maximum(total, floor_level))
    last = sends(
        mode, modes, mode_id, lambda peer: ratio_ref.at[mode], ratio_ref, send_r, recv_r
    )
    for copy in more + other:
        copy.wait()
    sum_ref[...] = jnp.sum(got_b[...], axis=0)
    for copy in last:
        copy.wait()


def inverse_kernel(
    sizes, places_ref, ratio_ref, far_ref, window_ref, probe_ref, rh, rl, gh, gl,
    terms_ref, mixed_ref,
):
    width = probe_ref.shape[0]
    block = terms_ref.shape[2]
    tiles = sizes[1]
    count = sizes[0] * tiles
    me = lax.axis_index("scan") * tiles + lax.axis_index("tile")
    start, _ = place_of(places_ref, me, block)
    ratio = ratio_ref[...]
    scaled = far_ref[...] * jnp.concatenate([ratio, ratio], 1)
    waves = left_product(rh[...], rl[...], right_product(scaled, gh[...], gl[...]))
    probe, window = probe_ref[...], window_ref[...]
    difference = waves - times(probe, window)
    terms = conj_times(probe, difference)
    for index in range(width // block):
        owner = lax.rem(start + index, count)
        terms_ref[owner, index // count] = terms[index * block : (index + 1) * block]
    mixed_ref[...] = conj_times(window, difference)


def reduce_kernel(
    sizes, places_ref, terms_ref, mixed_ref, probe_ref, square_ref, bright_ref, object_ref,
    out_ref, next_ref,
    got_t, got_p, canvas, got_c,
    send_t, recv_t, send_m, recv_m, send_c, recv_c, send_o, recv_o, send_n, recv_n,
):
    scans, tiles, modes = sizes
    count = scans * tiles
    rounds, block, width2 = terms_ref.shape[1:]
    width = width2 // 2
    columns = object_ref.shape[-1]
    scan, tile, mode = lax.axis_index("scan"), lax.axis_index("tile"), lax.axis_index("mode")
    me = scan * tiles + tile
    cycle = scan + scans * mode
    id_of = functools.partial(pattern_id, tiles)
    id_round = functools.partial(round_id, scans)
    greet([(me, count, id_of), (cycle, scans * modes, id_round)])
    moves_t = sends(me, count, id_of, lambda peer: terms_ref.at[peer], got_t, send_t, recv_t)
    got_t[me] = terms_ref[me]
    got_p[me] = mixed_ref[me]
    blank = jnp.zeros((block, columns - width), f32)
    zero = jnp.zeros((block, columns), f32)

    def spread(piece, col):
        return pltpu.roll(jnp.concatenate([piece, blank], 1), col, 1)

    weight = zero
    for index in range(count):
        start, col = place_of(places_ref, index, block)
        which = me + count * mode - start
        inside = jnp.logical_and(which >= 0, which < count * rounds)
        piece = square_ref[jnp.clip(which, 0, count * rounds - 1)]
        weight = weight + jnp.where(inside, spread(piece, col), 0.0)
    for copy in moves_t:
        copy.wait()
    moves_p = sends(me, count, id_of, lambda peer: mixed_ref.at[peer], got_p, send_m, recv_m)
    for part in range(2):
        sums = [zero] * modes
        for index in range(count):
            start, col = place_of(places_ref, index, block)
            first = (start + lax.rem(me - start + count * block * block, count)) // count
            for step in range(rounds):
                piece = spread(got_t[index, step, :, part * width : (part + 1) * width], col)
                for slot in range(modes):
                    sums[slot] = sums[slot] + jnp.where(first + step == slot, piece, 0.0)
        for slot in range(modes):
            canvas[slot, part] = sums[slot]
    moves_c = sends(mode, modes, mode_id, lambda peer: canvas.at[peer], got_c, send_c, recv_c)
    got_c[mode] = canvas[mode]
    for copy in moves_c:
        copy.wait()
    for part in range(2):
        total = got_c[0, part]
        for index in range(1, modes):
            total = total + got_c[index, part]
        out_ref[cycle, part] = object_ref[cycle, part] + total / (weight + damping)
    last = sends(
        cycle, scans * modes, id_round, lambda peer: out_ref.at[cycle], out_ref, send_o, recv_o
    )
    for copy in moves_p:
        copy.wait()
    totals = got_p[0]
    for index in range(1, count):
        totals = totals + got_p[index]
    divisor = bright_ref[...]
    next_ref[me] = probe_ref[me] + totals / jnp.concatenate([divisor, divisor], 1)
    last += sends(me, count, id_of, lambda peer: next_ref.at[me], next_ref, send_n, recv_n)
    for copy in last:
        copy.wait()


def shape(*dims):
    return jax.ShapeDtypeStruct(dims, f32)


def dma(count):
    return pltpu.SemaphoreType.DMA((count,))


def local(kernel, in_specs, outs, scratch=()):
    return pl.pallas_call(
        kernel,
        out_shape=outs,
        in_specs=in_specs,
        out_specs=jax.tree.map(lambda _: VMEM, outs),
        scratch_shapes=list(scratch),
        compiler_params=pltpu.CompilerParams(vmem_limit_bytes=vmem_bytes),
    )


def remote(kernel, number, inputs, outs, scratch):
    return pl.pallas_call(
        kernel,
        out_shape=outs,
        in_specs=inputs,
        out_specs=[VMEM] * len(outs),
        scratch_shapes=scratch,
        compiler_params=pltpu.CompilerParams(
            collective_id=number, has_side_effects=True, vmem_limit_bytes=vmem_bytes
        ),
    )


def one_wave(sizes, tables, object_field, probe_modes, intensities, positions):
    scans, tiles, modes = sizes
    count = scans * tiles
    width = probe_modes.shape[1]
    cycles, _, block, _, columns = object_field.shape
    blocks = width // block
    rounds = blocks // tiles
    share = width // count
    quarter = width // modes
    places = positions.T
    probe = probe_modes[0]
    planar = jnp.swapaxes(object_field[:, 0], 1, 2)
    got, squares = remote(
        functools.partial(fetch_kernel, sizes),
        0,
        [SMEM, VMEM, VMEM],
        [shape(tiles, rounds, 2, block, width), shape(modes, share, width)],
        [
            pltpu.VMEM((tiles, rounds, 2, block, width), f32),
            pltpu.VMEM((share, width), f32),
        ]
        + [dma(tiles - 1)] * 2
        + [dma(modes - 1)] * 2,
    )(places, planar, probe)
    window, far, strength, square, bright = local(
        functools.partial(forward_kernel, sizes),
        [SMEM] + [VMEM] * 7,
        [
            shape(width, 2 * width),
            shape(width, 2 * width),
            shape(width, width),
            shape(share, width),
            shape(width, width),
        ],
    )(places, got, squares, probe, *tables)
    ratio, squares, bright = remote(
        functools.partial(ratio_kernel, sizes),
        1,
        [VMEM] * 4,
        [shape(modes, quarter, width), shape(count, share, width), shape(share, width)],
        [pltpu.VMEM((modes, quarter, width), f32), pltpu.VMEM((count, share, width), f32)]
        + [dma(modes - 1)] * 4
        + [dma(count - 1)] * 4,
    )(
        strength.reshape(modes, quarter, width),
        square,
        bright.reshape(count, share, width),
        intensities.reshape(modes, quarter, width),
    )
    parts = blocks // count
    terms, mixed = local(
        functools.partial(inverse_kernel, sizes),
        [SMEM] + [VMEM] * 8,
        [shape(count, parts, block, 2 * width), shape(width, 2 * width)],
    )(places, ratio.reshape(width, width), far, window, probe, *tables)
    updated, probe_next = remote(
        functools.partial(reduce_kernel, sizes),
        2,
        [SMEM] + [VMEM] * 6,
        [shape(cycles, 2, block, columns), shape(count, share, 2 * width)],
        [
            pltpu.VMEM((count, parts, block, 2 * width), f32),
            pltpu.VMEM((count, share, 2 * width), f32),
            pltpu.VMEM((modes, 2, block, columns), f32),
            pltpu.VMEM((modes, 2, block, columns), f32),
        ]
        + [dma(count - 1)] * 4
        + [dma(modes - 1)] * 2
        + [dma(cycles - 1)] * 2
        + [dma(count - 1)] * 2,
    )(
        places,
        terms,
        mixed.reshape(count, share, 2 * width),
        probe.reshape(count, share, 2 * width),
        squares.reshape(blocks, block, width),
        bright,
        planar,
    )
    new_object = jnp.swapaxes(updated, 1, 2)[:, None]
    return (new_object, probe_next.reshape(1, width, 2 * width))


def solution(mesh):
    in_specs = (
        P(None, "tile", None, None, None),
        P("mode", None, None),
        P(("scan", "tile"), None, None),
        P(),
    )
    out_specs = (P(None, "tile", None, None, None), P("mode", None, None))
    sizes = (mesh.shape["scan"], mesh.shape["tile"], mesh.shape["mode"])

    def run(object_field, probe_modes, intensities, positions):
        body = on_device
        if (
            object_field.shape[0] == sizes[0] * sizes[2]
            and probe_modes.shape[0] == sizes[2]
            and intensities.shape[0] == sizes[0] * sizes[1]
            and probe_modes.shape[1] % (object_field.shape[2] * sizes[0] * sizes[1]) == 0
        ):
            tables = [jnp.asarray(table) for table in split_tables(probe_modes.shape[1])]
            body = functools.partial(one_wave, sizes, tables)
        return jax.shard_map(
            body, mesh=mesh, in_specs=in_specs, out_specs=out_specs, check_vma=False
        )(object_field, probe_modes, intensities, positions)

    return run
```

```python
import functools
import math

import jax
import jax.numpy as jnp
import ml_dtypes
import numpy as np
from jax import lax
from jax.experimental import pallas as pl
from jax.experimental.pallas import tpu as pltpu
from jax.sharding import PartitionSpec as P

floor_level = 0.1
damping = 1.0
highest = lax.Precision.HIGHEST


def transform_tables(width):
    index = jnp.arange(width, dtype=jnp.int32)
    phase = (index[:, None] * index[None, :] % width).astype(jnp.float32)
    angle = phase * (2.0 * math.pi / width)
    cosine = jnp.cos(angle) / math.sqrt(width)
    sine = -jnp.sin(angle) / math.sqrt(width)
    forward_rows = jnp.block([[cosine, sine], [-sine, cosine]])
    inverse_rows = jnp.block([[cosine, -sine], [sine, cosine]])
    return (cosine, sine, forward_rows, inverse_rows)


def times(left, right):
    half = left.shape[-1] // 2
    return jnp.concatenate(
        [
            left[..., :half] * right[..., :half] - left[..., half:] * right[..., half:],
            left[..., :half] * right[..., half:] + left[..., half:] * right[..., :half],
        ],
        -1,
    )


def conj_times(left, right):
    half = left.shape[-1] // 2
    return jnp.concatenate(
        [
            left[..., :half] * right[..., :half] + left[..., half:] * right[..., half:],
            left[..., :half] * right[..., half:] - left[..., half:] * right[..., :half],
        ],
        -1,
    )


def power(values):
    half = values.shape[-1] // 2
    return values[..., :half] ** 2 + values[..., half:] ** 2


def columns_forward(cosine, sine, data):
    half = data.shape[-1] // 2
    first = jnp.einsum("ab,pbc->pac", cosine, data, precision=highest)
    second = jnp.einsum("ab,pbc->pac", sine, data, precision=highest)
    return jnp.concatenate(
        [first[..., :half] - second[..., half:], first[..., half:] + second[..., :half]], -1
    )


def columns_inverse(cosine, sine, data):
    half = data.shape[-1] // 2
    first = jnp.einsum("ab,pbc->pac", cosine, data, precision=highest)
    second = jnp.einsum("ab,pbc->pac", sine, data, precision=highest)
    return jnp.concatenate(
        [first[..., :half] + second[..., half:], first[..., half:] - second[..., :half]], -1
    )


def project(cosine, sine, spectra, intensities):
    far_field = columns_forward(cosine, sine, spectra)
    total_power = lax.psum(power(far_field), "mode")
    ratio_map = jnp.sqrt(intensities / jnp.maximum(total_power, floor_level))
    return columns_inverse(cosine, sine, far_field * jnp.concatenate([ratio_map, ratio_map], -1))


def pick_rows(rows, picks):
    return rows[picks]


def assemble(received, order):
    moved = jnp.swapaxes(received, 0, 1)
    picked = jax.vmap(pick_rows)(moved, order)
    ordered = jnp.swapaxes(picked, 1, 2)
    return ordered.reshape(ordered.shape[0], -1, ordered.shape[-1])


def disassemble(ordered, order):
    moved = jnp.swapaxes(ordered, 1, 2)
    picked = jax.vmap(pick_rows)(moved, order)
    return jnp.swapaxes(picked, 0, 1)


def place(cycle_flat, col_flat, terms, weights, shape):
    cycle_count, block, columns = shape
    count, rows, doubled = terms.shape
    width = doubled // 2
    span = jnp.arange(width, dtype=jnp.int32)
    split_terms = terms.reshape(count, rows, 2, width)
    numerator = jnp.zeros((cycle_count, block, 2, columns), jnp.float32)
    numerator = numerator.at[
        cycle_flat[:, None, None, None],
        jnp.arange(rows, dtype=jnp.int32)[None, :, None, None],
        jnp.arange(2, dtype=jnp.int32)[None, None, :, None],
        col_flat[:, None, None, None] + span,
    ].add(split_terms)
    weight = jnp.zeros((cycle_count, block, columns), jnp.float32)
    weight = weight.at[
        cycle_flat[:, None, None],
        jnp.arange(block, dtype=jnp.int32)[None, :, None],
        col_flat[:, None, None] + span,
    ].add(weights)
    return (numerator, weight)


def on_device(object_field, probe_modes, intensities, positions):
    width = probe_modes.shape[1]
    cycles = object_field.shape[0]
    block = object_field.shape[2]
    columns = object_field.shape[4]
    tiles = lax.axis_size("tile")
    patterns = intensities.shape[0]
    blocks = width // block
    rounds = blocks // tiles
    scan_index = lax.axis_index("scan")
    tile_index = lax.axis_index("tile")
    group = lax.dynamic_slice_in_dim(
        positions, scan_index * (tiles * patterns), tiles * patterns, 0
    )
    group = group.reshape(tiles, patterns, 2)
    start_blocks = group[:, :, 0] // block
    start_cols = group[:, :, 1]
    own_starts = lax.dynamic_index_in_dim(start_blocks, tile_index, 0, keepdims=False)
    first_block = jnp.mod(tile_index - start_blocks, tiles)
    patch_blocks = first_block[:, :, None] + tiles * jnp.arange(rounds, dtype=jnp.int32)
    cycle_flat = ((start_blocks[:, :, None] + patch_blocks) // tiles).reshape(-1)
    col_flat = jnp.broadcast_to(start_cols[:, :, None], patch_blocks.shape).reshape(-1)
    patch_flat = patch_blocks.reshape(-1)
    count = patch_flat.shape[0]
    lanes = jnp.arange(tiles, dtype=jnp.int32)
    gather_order = jnp.mod(lanes[None, :] + own_starts[:, None], tiles)
    scatter_order = jnp.mod(lanes[None, :] - own_starts[:, None], tiles)
    cosine, sine, forward_rows, inverse_rows = transform_tables(width)
    selector = (patch_flat[None, :] == jnp.arange(blocks, dtype=jnp.int32)[:, None]).astype(
        jnp.float32
    )
    current = object_field[:, 0]
    probe_now = probe_modes[0]

    def cut(cycle, column):
        piece = lax.dynamic_slice(current, (cycle, 0, 0, column), (1, block, 2, width))
        return piece.reshape(block, 2 * width)

    object_rows = jax.vmap(cut)(cycle_flat, col_flat)
    probe_rows = probe_now.reshape(blocks, block, 2 * width)[patch_flat]
    exit_rows = times(probe_rows, object_rows)
    spectra = jnp.dot(exit_rows.reshape(-1, 2 * width), forward_rows, precision=highest)
    arrived = lax.all_to_all(
        spectra.reshape(tiles, patterns, rounds, block, 2 * width),
        "tile",
        split_axis=0,
        concat_axis=0,
        tiled=True,
    )
    returned = project(cosine, sine, assemble(arrived, gather_order), intensities)
    outgoing = disassemble(
        returned.reshape(patterns, rounds, tiles, block, 2 * width), scatter_order
    )
    came_back = lax.all_to_all(outgoing, "tile", split_axis=0, concat_axis=0, tiled=True)
    new_rows = jnp.dot(came_back.reshape(-1, 2 * width), inverse_rows, precision=highest)
    difference = new_rows.reshape(count, block, 2 * width) - exit_rows
    terms = conj_times(probe_rows, difference)
    mixed = jnp.concatenate([conj_times(object_rows, difference), power(object_rows)], -1)
    probe_stats = jnp.dot(selector, mixed.reshape(count, -1), precision=highest).reshape(
        width, 3 * width
    )
    numerator, weight = place(
        cycle_flat, col_flat, terms, power(probe_rows), (cycles, block, columns)
    )
    numerator, weight = lax.psum((numerator, weight), ("scan", "mode"))
    summed = lax.psum(probe_stats, ("scan", "tile"))
    divisor = summed[:, 2 * width :]
    probe_next = probe_now + summed[:, : 2 * width] / jnp.concatenate([divisor, divisor], -1)
    current = current + numerator / (weight[:, :, None, :] + damping)
    return (current[:, None], probe_next[None])


MESH = pl.DeviceIdType.MESH
VMEM = pl.BlockSpec(memory_space=pltpu.VMEM)
SMEM = pl.BlockSpec(memory_space=pltpu.SMEM)
vmem_bytes = 40 * 1024 * 1024
f32 = jnp.float32


def split_tables(width):
    index = np.arange(width)
    angle = (index[:, None] * index[None, :] % width) * (2.0 * math.pi / width)
    cosine = np.cos(angle) / math.sqrt(width)
    sine = -np.sin(angle) / math.sqrt(width)
    right = np.block([[cosine, sine], [-sine, cosine]])
    parts = []
    for table in (right, right.T):
        high = table.astype(ml_dtypes.bfloat16)
        low = (table - high.astype(np.float64)).astype(ml_dtypes.bfloat16)
        parts += [high, low]
    return parts


def halves(values):
    high = values.astype(jnp.bfloat16)
    return high, (values - high.astype(f32)).astype(jnp.bfloat16)


def dot(left, right):
    return jnp.dot(left, right, preferred_element_type=f32)


def right_product(values, high_table, low_table):
    high, low = halves(values)
    return dot(high, high_table) + (dot(low, high_table) + dot(high, low_table))


def left_product(high_table, low_table, values):
    half = values.shape[-1] // 2
    high, low = halves(jnp.concatenate([values[:, :half], values[:, half:]], 0))
    out = dot(high_table, high) + (dot(high_table, low) + dot(low_table, high))
    rows = out.shape[0] // 2
    return jnp.concatenate([out[:rows], out[rows:]], 1)


def sends(me, count, id_of, src_of, dst, send, recv):
    copies = []
    for step in range(1, count):
        peer = lax.rem(me + step, count)
        copies.append(
            pltpu.make_async_remote_copy(
                src_ref=src_of(peer),
                dst_ref=dst.at[me],
                send_sem=send.at[step - 1],
                recv_sem=recv.at[step - 1],
                device_id=id_of(peer),
                device_id_type=MESH,
            )
        )
    for copy in copies:
        copy.start()
    return copies


def greet(groups):
    barrier = pltpu.get_barrier_semaphore()
    total = 0
    for me, count, id_of in groups:
        for step in range(1, count):
            pl.semaphore_signal(
                barrier, inc=1, device_id=id_of(lax.rem(me + step, count)), device_id_type=MESH
            )
            total += 1
    pl.semaphore_wait(barrier, total)


def tile_id(peer):
    return {"tile": peer}


def mode_id(peer):
    return {"mode": peer}


def pattern_id(tiles, peer):
    return {"scan": peer // tiles, "tile": lax.rem(peer, tiles)}


def round_id(scans, peer):
    return {"scan": lax.rem(peer, scans), "mode": peer // scans}


def place_of(places_ref, index, block):
    return places_ref[0, index] // block, places_ref[1, index]


def fetch_kernel(
    sizes, places_ref, object_ref, probe_ref, got_ref, squares_ref,
    rows, square, send, recv, send_p, recv_p,
):
    scans, tiles, modes = sizes
    scan, tile, mode = lax.axis_index("scan"), lax.axis_index("tile"), lax.axis_index("mode")
    block = object_ref.shape[2]
    columns = object_ref.shape[3]
    rounds, width = rows.shape[1], rows.shape[4]
    for index in range(tiles):
        start, col = place_of(places_ref, scan * tiles + index, block)
        first = (start + lax.rem(tile - start + tiles * block * block, tiles)) // tiles
        piece = object_ref[pl.ds(first, rounds)].reshape(rounds * 2 * block, columns)
        piece = pltpu.roll(piece, lax.rem(columns - col, columns), 1)[:, :width]
        rows[index] = piece.reshape(rounds, 2, block, width)
    share = square.shape[0]
    square[...] = power(probe_ref[pl.ds((scan * tiles + tile) * share, share)])
    me = scan * tiles + tile
    greet(
        [
            (me, scans * tiles, functools.partial(pattern_id, tiles)),
            (scan + scans * mode, scans * modes, functools.partial(round_id, scans)),
        ]
    )
    copies = sends(tile, tiles, tile_id, lambda peer: rows.at[peer], got_ref, send, recv)
    copies += sends(mode, modes, mode_id, lambda peer: square, squares_ref, send_p, recv_p)
    got_ref[tile] = rows[tile]
    squares_ref[mode] = square[...]
    for copy in copies:
        copy.wait()


def forward_kernel(
    sizes, places_ref, got_ref, squares_ref, probe_ref, rh, rl, gh, gl,
    window_ref, far_ref, power_ref, square_ref, bright_ref,
):
    width = probe_ref.shape[0]
    block = got_ref.shape[3]
    tiles = sizes[1]
    me = lax.axis_index("scan") * tiles + lax.axis_index("tile")
    start, _ = place_of(places_ref, me, block)
    for index in range(width // block):
        owner = lax.rem(start + index, tiles)
        for part in range(2):
            window_ref[index * block : (index + 1) * block, part * width : (part + 1) * width] = (
                got_ref[owner, index // tiles, part]
            )
    waves = times(probe_ref[...], window_ref[...])
    far = left_product(gh[...], gl[...], right_product(waves, rh[...], rl[...]))
    far_ref[...] = far
    power_ref[...] = power(far).reshape(power_ref.shape)
    square_ref[...] = jnp.sum(squares_ref[...], axis=0)
    bright_ref[...] = power(window_ref[...]).reshape(bright_ref.shape)


def ratio_kernel(
    sizes, power_ref, square_ref, bright_ref, measured_ref, ratio_ref, squares_ref, sum_ref,
    got, got_b, send, recv, send_r, recv_r, send_p, recv_p, send_b, recv_b,
):
    scans, tiles, modes = sizes
    mode = lax.axis_index("mode")
    me = lax.axis_index("scan") * tiles + lax.axis_index("tile")
    id_of = functools.partial(pattern_id, tiles)
    first = sends(mode, modes, mode_id, lambda peer: power_ref.at[peer], got, send, recv)
    other = sends(me, scans * tiles, id_of, lambda peer: square_ref, squares_ref, send_p, recv_p)
    more = sends(
        me, scans * tiles, id_of, lambda peer: bright_ref.at[peer], got_b, send_b, recv_b
    )
    got_b[me] = bright_ref[me]
    got[mode] = power_ref[mode]
    squares_ref[me] = square_ref[...]
    for copy in first:
        copy.wait()
    total = got[0]
    for index in range(1, modes):
        total = total + got[index]
    ratio_ref[mode] = jnp.sqrt(measured_ref[mode] / jnp.maximum(total, floor_level))
    last = sends(
        mode, modes, mode_id, lambda peer: ratio_ref.at[mode], ratio_ref, send_r, recv_r
    )
    for copy in more + other:
        copy.wait()
    sum_ref[...] = jnp.sum(got_b[...], axis=0)
    for copy in last:
        copy.wait()


def inverse_kernel(
    sizes, places_ref, ratio_ref, far_ref, window_ref, probe_ref, rh, rl, gh, gl,
    terms_ref, mixed_ref, ordered,
):
    width = probe_ref.shape[0]
    block = terms_ref.shape[2]
    tiles = sizes[1]
    count = sizes[0] * tiles
    me = lax.axis_index("scan") * tiles + lax.axis_index("tile")
    start, _ = place_of(places_ref, me, block)
    ratio = ratio_ref[...].reshape(width, width)
    scaled = far_ref[...] * jnp.concatenate([ratio, ratio], 1)
    waves = left_product(rh[...], rl[...], right_product(scaled, gh[...], gl[...]))
    probe, window = probe_ref[...], window_ref[...]
    difference = waves - times(probe, window)
    terms = conj_times(probe, difference)
    ordered[...] = terms.reshape(ordered.shape)
    for owner in range(count):
        first = lax.rem(owner - start + count * block * block, count)
        for index in range(terms_ref.shape[1]):
            terms_ref[owner, index] = ordered[first + count * index]
    mixed_ref[...] = conj_times(window, difference).reshape(mixed_ref.shape)


def reduce_kernel(
    sizes, places_ref, terms_ref, mixed_ref, probe_ref, square_ref, bright_ref, object_ref,
    out_ref, next_ref,
    got_t, got_p, canvas, got_c,
    send_t, recv_t, send_m, recv_m, send_c, recv_c, send_o, recv_o, send_n, recv_n,
):
    scans, tiles, modes = sizes
    count = scans * tiles
    rounds, block, width2 = terms_ref.shape[1:]
    width = width2 // 2
    columns = object_ref.shape[-1]
    share = got_p.shape[1]
    scan, tile, mode = lax.axis_index("scan"), lax.axis_index("tile"), lax.axis_index("mode")
    me = scan * tiles + tile
    cycle = scan + scans * mode
    id_of = functools.partial(pattern_id, tiles)
    id_round = functools.partial(round_id, scans)
    moves_t = sends(me, count, id_of, lambda peer: terms_ref.at[peer], got_t, send_t, recv_t)
    got_t[me] = terms_ref[me]
    got_p[me] = mixed_ref[me]
    blank = jnp.zeros((block, columns - width), f32)
    zero = jnp.zeros((block, columns), f32)

    def spread(piece, col):
        return pltpu.roll(jnp.concatenate([piece, blank], 1), col, 1)

    weight = zero
    for index in range(count):
        start, col = place_of(places_ref, index, block)
        which = me + count * mode - start
        inside = jnp.logical_and(which >= 0, which < count * rounds)
        piece = square_ref[jnp.clip(which, 0, count * rounds - 1)]
        weight = weight + jnp.where(inside, spread(piece, col), 0.0)
    for copy in moves_t:
        copy.wait()
    moves_p = sends(me, count, id_of, lambda peer: mixed_ref.at[peer], got_p, send_m, recv_m)
    for part in range(2):
        sums = [zero] * modes
        for index in range(count):
            start, col = place_of(places_ref, index, block)
            first = (start + lax.rem(me - start + count * block * block, count)) // count
            for step in range(rounds):
                piece = spread(got_t[index, step, :, part * width : (part + 1) * width], col)
                for slot in range(modes):
                    sums[slot] = sums[slot] + jnp.where(first + step == slot, piece, 0.0)
        for slot in range(modes):
            canvas[slot, part] = sums[slot]
    moves_c = sends(mode, modes, mode_id, lambda peer: canvas.at[peer], got_c, send_c, recv_c)
    got_c[mode] = canvas[mode]
    for copy in moves_c:
        copy.wait()
    for part in range(2):
        total = got_c[0, part]
        for index in range(1, modes):
            total = total + got_c[index, part]
        out_ref[cycle, part] = object_ref[cycle, part] + total / (weight + damping)
    last = sends(
        cycle, scans * modes, id_round, lambda peer: out_ref.at[cycle], out_ref, send_o, recv_o
    )
    for copy in moves_p:
        copy.wait()
    totals = got_p[0]
    for index in range(1, count):
        totals = totals + got_p[index]
    divisor = bright_ref[...]
    next_ref[me] = probe_ref[pl.ds(me * share, share)] + totals / jnp.concatenate([divisor, divisor], 1)
    last += sends(me, count, id_of, lambda peer: next_ref.at[me], next_ref, send_n, recv_n)
    for copy in last:
        copy.wait()


def wave_kernel(
    sizes, places_ref, object_ref, probe_ref, measured_ref, rh, rl, gh, gl, out_ref, next_ref,
    rows, square, got_w, squares_m, window, far, strength, square_m, bright,
    ratio, squares, bright_sum, got_s, got_b, terms, mixed, ordered, squares_b,
    got_t, got_p, canvas, got_c, *sems,
):
    fetch_kernel(
        sizes, places_ref, object_ref, probe_ref, got_w, squares_m, rows, square, *sems[:4]
    )
    forward_kernel(
        sizes, places_ref, got_w, squares_m, probe_ref, rh, rl, gh, gl,
        window, far, strength, square_m, bright,
    )
    ratio_kernel(
        sizes, strength, square_m, bright, measured_ref, ratio, squares, bright_sum,
        got_s, got_b, *sems[4:12],
    )
    inverse_kernel(
        sizes, places_ref, ratio, far, window, probe_ref, rh, rl, gh, gl,
        terms, mixed, ordered,
    )
    squares_b[...] = squares[...].reshape(squares_b.shape)
    reduce_kernel(
        sizes, places_ref, terms, mixed, probe_ref, squares_b, bright_sum, object_ref,
        out_ref, next_ref, got_t, got_p, canvas, got_c, *sems[12:],
    )


def shape(*dims):
    return jax.ShapeDtypeStruct(dims, f32)


def dma(count):
    return pltpu.SemaphoreType.DMA((count,))


def one_wave(sizes, tables, object_field, probe_modes, intensities, positions):
    scans, tiles, modes = sizes
    count = scans * tiles
    width = probe_modes.shape[1]
    cycles, _, block, _, columns = object_field.shape
    blocks = width // block
    rounds = blocks // tiles
    parts = blocks // count
    share = width // count
    quarter = width // modes
    planar = jnp.swapaxes(object_field[:, 0], 1, 2)
    buffers = [
        (tiles, rounds, 2, block, width),
        (share, width),
        (tiles, rounds, 2, block, width),
        (modes, share, width),
        (width, 2 * width),
        (width, 2 * width),
        (modes, quarter, width),
        (share, width),
        (count, share, width),
        (modes, quarter, width),
        (count, share, width),
        (share, width),
        (modes, quarter, width),
        (count, share, width),
        (count, parts, block, 2 * width),
        (count, share, 2 * width),
        (blocks, block, 2 * width),
        (blocks, block, width),
        (count, parts, block, 2 * width),
        (count, share, 2 * width),
        (modes, 2, block, columns),
        (modes, 2, block, columns),
    ]
    peers = [tiles] * 2 + [modes] * 6 + [count] * 8 + [modes] * 2 + [cycles] * 2 + [count] * 2
    updated, probe_next = pl.pallas_call(
        functools.partial(wave_kernel, sizes),
        out_shape=[shape(cycles, 2, block, columns), shape(count, share, 2 * width)],
        in_specs=[SMEM] + [VMEM] * 7,
        out_specs=[VMEM] * 2,
        scratch_shapes=[pltpu.VMEM(dims, f32) for dims in buffers]
        + [dma(peer - 1) for peer in peers],
        compiler_params=pltpu.CompilerParams(
            collective_id=0, has_side_effects=True, vmem_limit_bytes=vmem_bytes
        ),
    )(
        positions.T,
        planar,
        probe_modes[0],
        intensities.reshape(modes, quarter, width),
        *tables,
    )
    new_object = jnp.swapaxes(updated, 1, 2)[:, None]
    return (new_object, probe_next.reshape(1, width, 2 * width))


def solution(mesh):
    in_specs = (
        P(None, "tile", None, None, None),
        P("mode", None, None),
        P(("scan", "tile"), None, None),
        P(),
    )
    out_specs = (P(None, "tile", None, None, None), P("mode", None, None))
    sizes = (mesh.shape["scan"], mesh.shape["tile"], mesh.shape["mode"])

    def run(object_field, probe_modes, intensities, positions):
        body = on_device
        if (
            object_field.shape[0] == sizes[0] * sizes[2]
            and probe_modes.shape[0] == sizes[2]
            and intensities.shape[0] == sizes[0] * sizes[1]
            and probe_modes.shape[1] % (object_field.shape[2] * sizes[0] * sizes[1]) == 0
        ):
            tables = [jnp.asarray(table) for table in split_tables(probe_modes.shape[1])]
            body = functools.partial(one_wave, sizes, tables)
        return jax.shard_map(
            body, mesh=mesh, in_specs=in_specs, out_specs=out_specs, check_vma=False
        )(object_field, probe_modes, intensities, positions)

    return run
```

```python
import functools
import math

import jax
import jax.numpy as jnp
import ml_dtypes
import numpy as np
from jax import lax
from jax.experimental import pallas as pl
from jax.experimental.pallas import tpu as pltpu
from jax.sharding import PartitionSpec as P

floor_level = 0.1
damping = 1.0
highest = lax.Precision.HIGHEST


def transform_tables(width):
    index = jnp.arange(width, dtype=jnp.int32)
    phase = (index[:, None] * index[None, :] % width).astype(jnp.float32)
    angle = phase * (2.0 * math.pi / width)
    cosine = jnp.cos(angle) / math.sqrt(width)
    sine = -jnp.sin(angle) / math.sqrt(width)
    forward_rows = jnp.block([[cosine, sine], [-sine, cosine]])
    inverse_rows = jnp.block([[cosine, -sine], [sine, cosine]])
    return (cosine, sine, forward_rows, inverse_rows)


def times(left, right):
    half = left.shape[-1] // 2
    return jnp.concatenate(
        [
            left[..., :half] * right[..., :half] - left[..., half:] * right[..., half:],
            left[..., :half] * right[..., half:] + left[..., half:] * right[..., :half],
        ],
        -1,
    )


def conj_times(left, right):
    half = left.shape[-1] // 2
    return jnp.concatenate(
        [
            left[..., :half] * right[..., :half] + left[..., half:] * right[..., half:],
            left[..., :half] * right[..., half:] - left[..., half:] * right[..., :half],
        ],
        -1,
    )


def power(values):
    half = values.shape[-1] // 2
    return values[..., :half] ** 2 + values[..., half:] ** 2


def columns_forward(cosine, sine, data):
    half = data.shape[-1] // 2
    first = jnp.einsum("ab,pbc->pac", cosine, data, precision=highest)
    second = jnp.einsum("ab,pbc->pac", sine, data, precision=highest)
    return jnp.concatenate(
        [first[..., :half] - second[..., half:], first[..., half:] + second[..., :half]], -1
    )


def columns_inverse(cosine, sine, data):
    half = data.shape[-1] // 2
    first = jnp.einsum("ab,pbc->pac", cosine, data, precision=highest)
    second = jnp.einsum("ab,pbc->pac", sine, data, precision=highest)
    return jnp.concatenate(
        [first[..., :half] + second[..., half:], first[..., half:] - second[..., :half]], -1
    )


def project(cosine, sine, spectra, intensities):
    far_field = columns_forward(cosine, sine, spectra)
    total_power = lax.psum(power(far_field), "mode")
    ratio_map = jnp.sqrt(intensities / jnp.maximum(total_power, floor_level))
    return columns_inverse(cosine, sine, far_field * jnp.concatenate([ratio_map, ratio_map], -1))


def pick_rows(rows, picks):
    return rows[picks]


def assemble(received, order):
    moved = jnp.swapaxes(received, 0, 1)
    picked = jax.vmap(pick_rows)(moved, order)
    ordered = jnp.swapaxes(picked, 1, 2)
    return ordered.reshape(ordered.shape[0], -1, ordered.shape[-1])


def disassemble(ordered, order):
    moved = jnp.swapaxes(ordered, 1, 2)
    picked = jax.vmap(pick_rows)(moved, order)
    return jnp.swapaxes(picked, 0, 1)


def place(cycle_flat, col_flat, terms, weights, shape):
    cycle_count, block, columns = shape
    count, rows, doubled = terms.shape
    width = doubled // 2
    span = jnp.arange(width, dtype=jnp.int32)
    split_terms = terms.reshape(count, rows, 2, width)
    numerator = jnp.zeros((cycle_count, block, 2, columns), jnp.float32)
    numerator = numerator.at[
        cycle_flat[:, None, None, None],
        jnp.arange(rows, dtype=jnp.int32)[None, :, None, None],
        jnp.arange(2, dtype=jnp.int32)[None, None, :, None],
        col_flat[:, None, None, None] + span,
    ].add(split_terms)
    weight = jnp.zeros((cycle_count, block, columns), jnp.float32)
    weight = weight.at[
        cycle_flat[:, None, None],
        jnp.arange(block, dtype=jnp.int32)[None, :, None],
        col_flat[:, None, None] + span,
    ].add(weights)
    return (numerator, weight)


def on_device(object_field, probe_modes, intensities, positions):
    width = probe_modes.shape[1]
    cycles = object_field.shape[0]
    block = object_field.shape[2]
    columns = object_field.shape[4]
    tiles = lax.axis_size("tile")
    patterns = intensities.shape[0]
    blocks = width // block
    rounds = blocks // tiles
    scan_index = lax.axis_index("scan")
    tile_index = lax.axis_index("tile")
    group = lax.dynamic_slice_in_dim(
        positions, scan_index * (tiles * patterns), tiles * patterns, 0
    )
    group = group.reshape(tiles, patterns, 2)
    start_blocks = group[:, :, 0] // block
    start_cols = group[:, :, 1]
    own_starts = lax.dynamic_index_in_dim(start_blocks, tile_index, 0, keepdims=False)
    first_block = jnp.mod(tile_index - start_blocks, tiles)
    patch_blocks = first_block[:, :, None] + tiles * jnp.arange(rounds, dtype=jnp.int32)
    cycle_flat = ((start_blocks[:, :, None] + patch_blocks) // tiles).reshape(-1)
    col_flat = jnp.broadcast_to(start_cols[:, :, None], patch_blocks.shape).reshape(-1)
    patch_flat = patch_blocks.reshape(-1)
    count = patch_flat.shape[0]
    lanes = jnp.arange(tiles, dtype=jnp.int32)
    gather_order = jnp.mod(lanes[None, :] + own_starts[:, None], tiles)
    scatter_order = jnp.mod(lanes[None, :] - own_starts[:, None], tiles)
    cosine, sine, forward_rows, inverse_rows = transform_tables(width)
    selector = (patch_flat[None, :] == jnp.arange(blocks, dtype=jnp.int32)[:, None]).astype(
        jnp.float32
    )
    current = object_field[:, 0]
    probe_now = probe_modes[0]

    def cut(cycle, column):
        piece = lax.dynamic_slice(current, (cycle, 0, 0, column), (1, block, 2, width))
        return piece.reshape(block, 2 * width)

    object_rows = jax.vmap(cut)(cycle_flat, col_flat)
    probe_rows = probe_now.reshape(blocks, block, 2 * width)[patch_flat]
    exit_rows = times(probe_rows, object_rows)
    spectra = jnp.dot(exit_rows.reshape(-1, 2 * width), forward_rows, precision=highest)
    arrived = lax.all_to_all(
        spectra.reshape(tiles, patterns, rounds, block, 2 * width),
        "tile",
        split_axis=0,
        concat_axis=0,
        tiled=True,
    )
    returned = project(cosine, sine, assemble(arrived, gather_order), intensities)
    outgoing = disassemble(
        returned.reshape(patterns, rounds, tiles, block, 2 * width), scatter_order
    )
    came_back = lax.all_to_all(outgoing, "tile", split_axis=0, concat_axis=0, tiled=True)
    new_rows = jnp.dot(came_back.reshape(-1, 2 * width), inverse_rows, precision=highest)
    difference = new_rows.reshape(count, block, 2 * width) - exit_rows
    terms = conj_times(probe_rows, difference)
    mixed = jnp.concatenate([conj_times(object_rows, difference), power(object_rows)], -1)
    probe_stats = jnp.dot(selector, mixed.reshape(count, -1), precision=highest).reshape(
        width, 3 * width
    )
    numerator, weight = place(
        cycle_flat, col_flat, terms, power(probe_rows), (cycles, block, columns)
    )
    numerator, weight = lax.psum((numerator, weight), ("scan", "mode"))
    summed = lax.psum(probe_stats, ("scan", "tile"))
    divisor = summed[:, 2 * width :]
    probe_next = probe_now + summed[:, : 2 * width] / jnp.concatenate([divisor, divisor], -1)
    current = current + numerator / (weight[:, :, None, :] + damping)
    return (current[:, None], probe_next[None])


MESH = pl.DeviceIdType.MESH
VMEM = pl.BlockSpec(memory_space=pltpu.VMEM)
SMEM = pl.BlockSpec(memory_space=pltpu.SMEM)
vmem_bytes = 40 * 1024 * 1024
f32 = jnp.float32


def split_tables(width):
    index = np.arange(width)
    angle = (index[:, None] * index[None, :] % width) * (2.0 * math.pi / width)
    cosine = np.cos(angle) / math.sqrt(width)
    sine = -np.sin(angle) / math.sqrt(width)
    right = np.block([[cosine, sine], [-sine, cosine]])
    parts = []
    for table in (right, right.T):
        high = table.astype(ml_dtypes.bfloat16)
        low = (table - high.astype(np.float64)).astype(ml_dtypes.bfloat16)
        parts += [high, low]
    return parts


def halves(values):
    high = values.astype(jnp.bfloat16)
    return high, (values - high.astype(f32)).astype(jnp.bfloat16)


def dot(left, right):
    return jnp.dot(left, right, preferred_element_type=f32)


def right_product(values, high_table, low_table):
    high, low = halves(values)
    return dot(high, high_table) + (dot(low, high_table) + dot(high, low_table))


def left_product(high_table, low_table, values):
    half = values.shape[-1] // 2
    high, low = halves(jnp.concatenate([values[:, :half], values[:, half:]], 0))
    out = dot(high_table, high) + (dot(high_table, low) + dot(low_table, high))
    rows = out.shape[0] // 2
    return jnp.concatenate([out[:rows], out[rows:]], 1)


def sends(me, count, id_of, src_of, dst, send, recv):
    copies = []
    for step in range(1, count):
        peer = lax.rem(me + step, count)
        copies.append(
            pltpu.make_async_remote_copy(
                src_ref=src_of(peer),
                dst_ref=dst.at[me],
                send_sem=send.at[step - 1],
                recv_sem=recv.at[step - 1],
                device_id=id_of(peer),
                device_id_type=MESH,
            )
        )
    for copy in copies:
        copy.start()
    return copies


def greet(groups):
    barrier = pltpu.get_barrier_semaphore()
    total = 0
    for me, count, id_of in groups:
        for step in range(1, count):
            pl.semaphore_signal(
                barrier, inc=1, device_id=id_of(lax.rem(me + step, count)), device_id_type=MESH
            )
            total += 1
    pl.semaphore_wait(barrier, total)


def tile_id(peer):
    return {"tile": peer}


def mode_id(peer):
    return {"mode": peer}


def pattern_id(tiles, peer):
    return {"scan": peer // tiles, "tile": lax.rem(peer, tiles)}


def round_id(scans, peer):
    return {"scan": lax.rem(peer, scans), "mode": peer // scans}


def place_of(places_ref, index, block):
    return places_ref[0, index] // block, places_ref[1, index]


def fetch_kernel(
    sizes, places_ref, object_ref, probe_ref, got_ref, squares_ref,
    rows, square, send, recv, send_p, recv_p,
):
    scans, tiles, modes = sizes
    scan, tile, mode = lax.axis_index("scan"), lax.axis_index("tile"), lax.axis_index("mode")
    block = object_ref.shape[2]
    columns = object_ref.shape[3]
    rounds, width = rows.shape[1], rows.shape[4]
    for index in range(tiles):
        start, col = place_of(places_ref, scan * tiles + index, block)
        first = (start + lax.rem(tile - start + tiles * block * block, tiles)) // tiles
        piece = object_ref[pl.ds(first, rounds)].reshape(rounds * 2 * block, columns)
        piece = pltpu.roll(piece, lax.rem(columns - col, columns), 1)[:, :width]
        rows[index] = piece.reshape(rounds, 2, block, width)
    share = square.shape[0]
    square[...] = power(probe_ref[pl.ds((scan * tiles + tile) * share, share)])
    me = scan * tiles + tile
    greet(
        [
            (me, scans * tiles, functools.partial(pattern_id, tiles)),
            (scan + scans * mode, scans * modes, functools.partial(round_id, scans)),
        ]
    )
    copies = sends(tile, tiles, tile_id, lambda peer: rows.at[peer], got_ref, send, recv)
    copies += sends(mode, modes, mode_id, lambda peer: square, squares_ref, send_p, recv_p)
    got_ref[tile] = rows[tile]
    squares_ref[mode] = square[...]
    for copy in copies:
        copy.wait()


def forward_kernel(
    sizes, places_ref, got_ref, squares_ref, probe_ref, rh, rl, gh, gl,
    window_ref, far_ref, power_ref, square_ref, bright_ref,
):
    width = probe_ref.shape[0]
    block = got_ref.shape[3]
    tiles = sizes[1]
    me = lax.axis_index("scan") * tiles + lax.axis_index("tile")
    start, _ = place_of(places_ref, me, block)
    for index in range(width // block):
        owner = lax.rem(start + index, tiles)
        for part in range(2):
            window_ref[index * block : (index + 1) * block, part * width : (part + 1) * width] = (
                got_ref[owner, index // tiles, part]
            )
    waves = times(probe_ref[...], window_ref[...])
    far = left_product(gh[...], gl[...], right_product(waves, rh[...], rl[...]))
    far_ref[...] = far
    power_ref[...] = power(far).reshape(power_ref.shape)
    square_ref[...] = jnp.sum(squares_ref[...], axis=0)
    bright_ref[...] = power(window_ref[...]).reshape(bright_ref.shape)


def ratio_kernel(
    sizes, power_ref, square_ref, bright_ref, measured_ref, ratio_ref, squares_ref, sum_ref,
    got, got_b, send, recv, send_r, recv_r, send_p, recv_p, send_b, recv_b,
):
    scans, tiles, modes = sizes
    mode = lax.axis_index("mode")
    me = lax.axis_index("scan") * tiles + lax.axis_index("tile")
    id_of = functools.partial(pattern_id, tiles)
    first = sends(mode, modes, mode_id, lambda peer: power_ref.at[peer], got, send, recv)
    other = sends(me, scans * tiles, id_of, lambda peer: square_ref, squares_ref, send_p, recv_p)
    more = sends(
        me, scans * tiles, id_of, lambda peer: bright_ref.at[peer], got_b, send_b, recv_b
    )
    got_b[me] = bright_ref[me]
    got[mode] = power_ref[mode]
    squares_ref[me] = square_ref[...]
    for copy in first:
        copy.wait()
    total = got[0]
    for index in range(1, modes):
        total = total + got[index]
    ratio_ref[mode] = jnp.sqrt(measured_ref[mode] / jnp.maximum(total, floor_level))
    last = sends(
        mode, modes, mode_id, lambda peer: ratio_ref.at[mode], ratio_ref, send_r, recv_r
    )
    for copy in more + other:
        copy.wait()
    sum_ref[...] = jnp.sum(got_b[...], axis=0)
    for copy in last:
        copy.wait()


def inverse_kernel(
    sizes, places_ref, ratio_ref, far_ref, window_ref, probe_ref, rh, rl, gh, gl,
    terms_ref, mixed_ref, ordered,
):
    width = probe_ref.shape[0]
    block = terms_ref.shape[2]
    tiles = sizes[1]
    count = sizes[0] * tiles
    me = lax.axis_index("scan") * tiles + lax.axis_index("tile")
    start, _ = place_of(places_ref, me, block)
    ratio = ratio_ref[...].reshape(width, width)
    scaled = far_ref[...] * jnp.concatenate([ratio, ratio], 1)
    waves = left_product(rh[...], rl[...], right_product(scaled, gh[...], gl[...]))
    probe, window = probe_ref[...], window_ref[...]
    difference = waves - times(probe, window)
    terms = conj_times(probe, difference)
    ordered[...] = terms.reshape(ordered.shape)
    for owner in range(count):
        first = lax.rem(owner - start + count * block * block, count)
        for index in range(terms_ref.shape[1]):
            terms_ref[owner, index] = ordered[first + count * index]
    mixed_ref[...] = conj_times(window, difference).reshape(mixed_ref.shape)


def reduce_kernel(
    sizes, places_ref, terms_ref, mixed_ref, probe_ref, square_ref, bright_ref, object_ref,
    out_ref, next_ref,
    got_t, got_p, canvas, got_c,
    send_t, recv_t, send_m, recv_m, send_c, recv_c, send_o, recv_o, send_n, recv_n,
):
    scans, tiles, modes = sizes
    count = scans * tiles
    rounds, block, width2 = terms_ref.shape[1:]
    width = width2 // 2
    columns = object_ref.shape[-1]
    share = got_p.shape[1]
    scan, tile, mode = lax.axis_index("scan"), lax.axis_index("tile"), lax.axis_index("mode")
    me = scan * tiles + tile
    cycle = scan + scans * mode
    id_of = functools.partial(pattern_id, tiles)
    moves_t = sends(me, count, id_of, lambda peer: terms_ref.at[peer], got_t, send_t, recv_t)
    got_t[me] = terms_ref[me]
    got_p[me] = mixed_ref[me]
    blank = jnp.zeros((block, columns - width), f32)
    zero = jnp.zeros((block, columns), f32)

    def spread(piece, col):
        return pltpu.roll(jnp.concatenate([piece, blank], 1), col, 1)

    weight = zero
    for index in range(count):
        start, col = place_of(places_ref, index, block)
        which = me + count * mode - start
        inside = jnp.logical_and(which >= 0, which < count * rounds)
        piece = square_ref[jnp.clip(which, 0, count * rounds - 1)]
        weight = weight + jnp.where(inside, spread(piece, col), 0.0)
    for copy in moves_t:
        copy.wait()
    moves_p = sends(me, count, id_of, lambda peer: mixed_ref.at[peer], got_p, send_m, recv_m)
    for part in range(2):
        sums = [zero] * modes
        for index in range(count):
            start, col = place_of(places_ref, index, block)
            first = (start + lax.rem(me - start + count * block * block, count)) // count
            for step in range(rounds):
                piece = spread(got_t[index, step, :, part * width : (part + 1) * width], col)
                for slot in range(modes):
                    sums[slot] = sums[slot] + jnp.where(first + step == slot, piece, 0.0)
        for slot in range(modes):
            canvas[slot, part] = sums[slot]
    moves_c = sends(mode, modes, mode_id, lambda peer: canvas.at[peer], got_c, send_c, recv_c)
    got_c[mode] = canvas[mode]
    for copy in moves_c:
        copy.wait()
    for part in range(2):
        total = got_c[0, part]
        for index in range(1, modes):
            total = total + got_c[index, part]
        out_ref[cycle, part] = object_ref[cycle, part] + total / (weight + damping)

    def pass_on(at, slot, target):
        copy = pltpu.make_async_remote_copy(
            src_ref=out_ref.at[at],
            dst_ref=out_ref.at[at],
            send_sem=send_o.at[slot],
            recv_sem=recv_o.at[slot],
            device_id=target,
            device_id_type=MESH,
        )
        copy.start()
        return copy

    def across(step):
        at = scan + scans * lax.rem(mode - step + modes, modes)
        return [
            pass_on(
                at,
                modes - 1 + step * (scans - 1) + turn - 1,
                {"scan": lax.rem(scan + turn, scans)},
            )
            for turn in range(1, scans)
        ]

    along = [
        pass_on(cycle, step - 1, mode_id(lax.rem(mode + step, modes)))
        for step in range(1, modes)
    ]
    last = across(0)
    for copy in moves_p:
        copy.wait()
    totals = got_p[0]
    for index in range(1, count):
        totals = totals + got_p[index]
    divisor = bright_ref[...]
    next_ref[me] = probe_ref[pl.ds(me * share, share)] + totals / jnp.concatenate([divisor, divisor], 1)
    last += sends(me, count, id_of, lambda peer: next_ref.at[me], next_ref, send_n, recv_n)
    for step in range(1, modes):
        along[step - 1].wait_recv()
        last += across(step)
    for copy in along:
        copy.wait_send()
    for copy in last:
        copy.wait()


def wave_kernel(
    sizes, places_ref, object_ref, probe_ref, measured_ref, rh, rl, gh, gl, out_ref, next_ref,
    rows, square, got_w, squares_m, window, far, strength, square_m, bright,
    ratio, squares, bright_sum, got_s, got_b, terms, mixed, ordered, squares_b,
    got_t, got_p, canvas, got_c, *sems,
):
    fetch_kernel(
        sizes, places_ref, object_ref, probe_ref, got_w, squares_m, rows, square, *sems[:4]
    )
    forward_kernel(
        sizes, places_ref, got_w, squares_m, probe_ref, rh, rl, gh, gl,
        window, far, strength, square_m, bright,
    )
    ratio_kernel(
        sizes, strength, square_m, bright, measured_ref, ratio, squares, bright_sum,
        got_s, got_b, *sems[4:12],
    )
    inverse_kernel(
        sizes, places_ref, ratio, far, window, probe_ref, rh, rl, gh, gl,
        terms, mixed, ordered,
    )
    squares_b[...] = squares[...].reshape(squares_b.shape)
    reduce_kernel(
        sizes, places_ref, terms, mixed, probe_ref, squares_b, bright_sum, object_ref,
        out_ref, next_ref, got_t, got_p, canvas, got_c, *sems[12:],
    )


def shape(*dims):
    return jax.ShapeDtypeStruct(dims, f32)


def dma(count):
    return pltpu.SemaphoreType.DMA((count,))


def one_wave(sizes, tables, object_field, probe_modes, intensities, positions):
    scans, tiles, modes = sizes
    count = scans * tiles
    width = probe_modes.shape[1]
    cycles, _, block, _, columns = object_field.shape
    blocks = width // block
    rounds = blocks // tiles
    parts = blocks // count
    share = width // count
    quarter = width // modes
    planar = jnp.swapaxes(object_field[:, 0], 1, 2)
    buffers = [
        (tiles, rounds, 2, block, width),
        (share, width),
        (tiles, rounds, 2, block, width),
        (modes, share, width),
        (width, 2 * width),
        (width, 2 * width),
        (modes, quarter, width),
        (share, width),
        (count, share, width),
        (modes, quarter, width),
        (count, share, width),
        (share, width),
        (modes, quarter, width),
        (count, share, width),
        (count, parts, block, 2 * width),
        (count, share, 2 * width),
        (blocks, block, 2 * width),
        (blocks, block, width),
        (count, parts, block, 2 * width),
        (count, share, 2 * width),
        (modes, 2, block, columns),
        (modes, 2, block, columns),
    ]
    peers = [tiles] * 2 + [modes] * 6 + [count] * 8 + [modes] * 2 + [cycles] * 2 + [count] * 2
    updated, probe_next = pl.pallas_call(
        functools.partial(wave_kernel, sizes),
        out_shape=[shape(cycles, 2, block, columns), shape(count, share, 2 * width)],
        in_specs=[SMEM] + [VMEM] * 7,
        out_specs=[VMEM] * 2,
        scratch_shapes=[pltpu.VMEM(dims, f32) for dims in buffers]
        + [dma(peer - 1) for peer in peers],
        compiler_params=pltpu.CompilerParams(
            collective_id=0, has_side_effects=True, vmem_limit_bytes=vmem_bytes
        ),
    )(
        positions.T,
        planar,
        probe_modes[0],
        intensities.reshape(modes, quarter, width),
        *tables,
    )
    new_object = jnp.swapaxes(updated, 1, 2)[:, None]
    return (new_object, probe_next.reshape(1, width, 2 * width))


def solution(mesh):
    in_specs = (
        P(None, "tile", None, None, None),
        P("mode", None, None),
        P(("scan", "tile"), None, None),
        P(),
    )
    out_specs = (P(None, "tile", None, None, None), P("mode", None, None))
    sizes = (mesh.shape["scan"], mesh.shape["tile"], mesh.shape["mode"])

    def run(object_field, probe_modes, intensities, positions):
        body = on_device
        if (
            object_field.shape[0] == sizes[0] * sizes[2]
            and probe_modes.shape[0] == sizes[2]
            and intensities.shape[0] == sizes[0] * sizes[1]
            and probe_modes.shape[1] % (object_field.shape[2] * sizes[0] * sizes[1]) == 0
        ):
            tables = [jnp.asarray(table) for table in split_tables(probe_modes.shape[1])]
            body = functools.partial(one_wave, sizes, tables)
        return jax.shard_map(
            body, mesh=mesh, in_specs=in_specs, out_specs=out_specs, check_vma=False
        )(object_field, probe_modes, intensities, positions)

    return run
```

```python
import functools
import math

import jax
import jax.numpy as jnp
import ml_dtypes
import numpy as np
from jax import lax
from jax.experimental import pallas as pl
from jax.experimental.pallas import tpu as pltpu
from jax.sharding import PartitionSpec as P

floor_level = 0.1
damping = 1.0
highest = lax.Precision.HIGHEST


def transform_tables(width):
    index = jnp.arange(width, dtype=jnp.int32)
    phase = (index[:, None] * index[None, :] % width).astype(jnp.float32)
    angle = phase * (2.0 * math.pi / width)
    cosine = jnp.cos(angle) / math.sqrt(width)
    sine = -jnp.sin(angle) / math.sqrt(width)
    forward_rows = jnp.block([[cosine, sine], [-sine, cosine]])
    inverse_rows = jnp.block([[cosine, -sine], [sine, cosine]])
    return (cosine, sine, forward_rows, inverse_rows)


def times(left, right):
    half = left.shape[-1] // 2
    return jnp.concatenate(
        [
            left[..., :half] * right[..., :half] - left[..., half:] * right[..., half:],
            left[..., :half] * right[..., half:] + left[..., half:] * right[..., :half],
        ],
        -1,
    )


def conj_times(left, right):
    half = left.shape[-1] // 2
    return jnp.concatenate(
        [
            left[..., :half] * right[..., :half] + left[..., half:] * right[..., half:],
            left[..., :half] * right[..., half:] - left[..., half:] * right[..., :half],
        ],
        -1,
    )


def power(values):
    half = values.shape[-1] // 2
    return values[..., :half] ** 2 + values[..., half:] ** 2


def columns_forward(cosine, sine, data):
    half = data.shape[-1] // 2
    first = jnp.einsum("ab,pbc->pac", cosine, data, precision=highest)
    second = jnp.einsum("ab,pbc->pac", sine, data, precision=highest)
    return jnp.concatenate(
        [first[..., :half] - second[..., half:], first[..., half:] + second[..., :half]], -1
    )


def columns_inverse(cosine, sine, data):
    half = data.shape[-1] // 2
    first = jnp.einsum("ab,pbc->pac", cosine, data, precision=highest)
    second = jnp.einsum("ab,pbc->pac", sine, data, precision=highest)
    return jnp.concatenate(
        [first[..., :half] + second[..., half:], first[..., half:] - second[..., :half]], -1
    )


def project(cosine, sine, spectra, intensities):
    far_field = columns_forward(cosine, sine, spectra)
    total_power = lax.psum(power(far_field), "mode")
    ratio_map = jnp.sqrt(intensities / jnp.maximum(total_power, floor_level))
    return columns_inverse(cosine, sine, far_field * jnp.concatenate([ratio_map, ratio_map], -1))


def pick_rows(rows, picks):
    return rows[picks]


def assemble(received, order):
    moved = jnp.swapaxes(received, 0, 1)
    picked = jax.vmap(pick_rows)(moved, order)
    ordered = jnp.swapaxes(picked, 1, 2)
    return ordered.reshape(ordered.shape[0], -1, ordered.shape[-1])


def disassemble(ordered, order):
    moved = jnp.swapaxes(ordered, 1, 2)
    picked = jax.vmap(pick_rows)(moved, order)
    return jnp.swapaxes(picked, 0, 1)


def place(cycle_flat, col_flat, terms, weights, shape):
    cycle_count, block, columns = shape
    count, rows, doubled = terms.shape
    width = doubled // 2
    span = jnp.arange(width, dtype=jnp.int32)
    split_terms = terms.reshape(count, rows, 2, width)
    numerator = jnp.zeros((cycle_count, block, 2, columns), jnp.float32)
    numerator = numerator.at[
        cycle_flat[:, None, None, None],
        jnp.arange(rows, dtype=jnp.int32)[None, :, None, None],
        jnp.arange(2, dtype=jnp.int32)[None, None, :, None],
        col_flat[:, None, None, None] + span,
    ].add(split_terms)
    weight = jnp.zeros((cycle_count, block, columns), jnp.float32)
    weight = weight.at[
        cycle_flat[:, None, None],
        jnp.arange(block, dtype=jnp.int32)[None, :, None],
        col_flat[:, None, None] + span,
    ].add(weights)
    return (numerator, weight)


def on_device(object_field, probe_modes, intensities, positions):
    width = probe_modes.shape[1]
    cycles = object_field.shape[0]
    block = object_field.shape[2]
    columns = object_field.shape[4]
    tiles = lax.axis_size("tile")
    patterns = intensities.shape[0]
    blocks = width // block
    rounds = blocks // tiles
    scan_index = lax.axis_index("scan")
    tile_index = lax.axis_index("tile")
    group = lax.dynamic_slice_in_dim(
        positions, scan_index * (tiles * patterns), tiles * patterns, 0
    )
    group = group.reshape(tiles, patterns, 2)
    start_blocks = group[:, :, 0] // block
    start_cols = group[:, :, 1]
    own_starts = lax.dynamic_index_in_dim(start_blocks, tile_index, 0, keepdims=False)
    first_block = jnp.mod(tile_index - start_blocks, tiles)
    patch_blocks = first_block[:, :, None] + tiles * jnp.arange(rounds, dtype=jnp.int32)
    cycle_flat = ((start_blocks[:, :, None] + patch_blocks) // tiles).reshape(-1)
    col_flat = jnp.broadcast_to(start_cols[:, :, None], patch_blocks.shape).reshape(-1)
    patch_flat = patch_blocks.reshape(-1)
    count = patch_flat.shape[0]
    lanes = jnp.arange(tiles, dtype=jnp.int32)
    gather_order = jnp.mod(lanes[None, :] + own_starts[:, None], tiles)
    scatter_order = jnp.mod(lanes[None, :] - own_starts[:, None], tiles)
    cosine, sine, forward_rows, inverse_rows = transform_tables(width)
    selector = (patch_flat[None, :] == jnp.arange(blocks, dtype=jnp.int32)[:, None]).astype(
        jnp.float32
    )
    current = object_field[:, 0]
    probe_now = probe_modes[0]

    def cut(cycle, column):
        piece = lax.dynamic_slice(current, (cycle, 0, 0, column), (1, block, 2, width))
        return piece.reshape(block, 2 * width)

    object_rows = jax.vmap(cut)(cycle_flat, col_flat)
    probe_rows = probe_now.reshape(blocks, block, 2 * width)[patch_flat]
    exit_rows = times(probe_rows, object_rows)
    spectra = jnp.dot(exit_rows.reshape(-1, 2 * width), forward_rows, precision=highest)
    arrived = lax.all_to_all(
        spectra.reshape(tiles, patterns, rounds, block, 2 * width),
        "tile",
        split_axis=0,
        concat_axis=0,
        tiled=True,
    )
    returned = project(cosine, sine, assemble(arrived, gather_order), intensities)
    outgoing = disassemble(
        returned.reshape(patterns, rounds, tiles, block, 2 * width), scatter_order
    )
    came_back = lax.all_to_all(outgoing, "tile", split_axis=0, concat_axis=0, tiled=True)
    new_rows = jnp.dot(came_back.reshape(-1, 2 * width), inverse_rows, precision=highest)
    difference = new_rows.reshape(count, block, 2 * width) - exit_rows
    terms = conj_times(probe_rows, difference)
    mixed = jnp.concatenate([conj_times(object_rows, difference), power(object_rows)], -1)
    probe_stats = jnp.dot(selector, mixed.reshape(count, -1), precision=highest).reshape(
        width, 3 * width
    )
    numerator, weight = place(
        cycle_flat, col_flat, terms, power(probe_rows), (cycles, block, columns)
    )
    numerator, weight = lax.psum((numerator, weight), ("scan", "mode"))
    summed = lax.psum(probe_stats, ("scan", "tile"))
    divisor = summed[:, 2 * width :]
    probe_next = probe_now + summed[:, : 2 * width] / jnp.concatenate([divisor, divisor], -1)
    current = current + numerator / (weight[:, :, None, :] + damping)
    return (current[:, None], probe_next[None])


MESH = pl.DeviceIdType.MESH
VMEM = pl.BlockSpec(memory_space=pltpu.VMEM)
SMEM = pl.BlockSpec(memory_space=pltpu.SMEM)
vmem_bytes = 40 * 1024 * 1024
f32 = jnp.float32


def split_tables(width):
    index = np.arange(width)
    angle = (index[:, None] * index[None, :] % width) * (2.0 * math.pi / width)
    cosine = np.cos(angle) / math.sqrt(width)
    sine = -np.sin(angle) / math.sqrt(width)
    right = np.block([[cosine, sine], [-sine, cosine]])
    parts = []
    for table in (right, right.T):
        high = table.astype(ml_dtypes.bfloat16)
        low = (table - high.astype(np.float64)).astype(ml_dtypes.bfloat16)
        parts += [high, low]
    return parts


def halves(values):
    high = values.astype(jnp.bfloat16)
    return high, (values - high.astype(f32)).astype(jnp.bfloat16)


def dot(left, right):
    return jnp.dot(left, right, preferred_element_type=f32)


def right_product(values, high_table, low_table):
    high, low = halves(values)
    return dot(high, high_table) + (dot(low, high_table) + dot(high, low_table))


def left_product(high_table, low_table, values):
    half = values.shape[-1] // 2
    high, low = halves(jnp.concatenate([values[:, :half], values[:, half:]], 0))
    out = dot(high_table, high) + (dot(high_table, low) + dot(low_table, high))
    rows = out.shape[0] // 2
    return jnp.concatenate([out[:rows], out[rows:]], 1)


def sends(me, count, id_of, src_of, dst, send, recv):
    copies = []
    for step in range(1, count):
        peer = lax.rem(me + step, count)
        copies.append(
            pltpu.make_async_remote_copy(
                src_ref=src_of(peer),
                dst_ref=dst.at[me],
                send_sem=send.at[step - 1],
                recv_sem=recv.at[step - 1],
                device_id=id_of(peer),
                device_id_type=MESH,
            )
        )
    for copy in copies:
        copy.start()
    return copies


def greet(groups):
    barrier = pltpu.get_barrier_semaphore()
    total = 0
    for me, count, id_of in groups:
        for step in range(1, count):
            pl.semaphore_signal(
                barrier, inc=1, device_id=id_of(lax.rem(me + step, count)), device_id_type=MESH
            )
            total += 1
    return barrier, total


def tile_id(peer):
    return {"tile": peer}


def mode_id(peer):
    return {"mode": peer}


def pattern_id(tiles, peer):
    return {"scan": peer // tiles, "tile": lax.rem(peer, tiles)}


def round_id(scans, peer):
    return {"scan": lax.rem(peer, scans), "mode": peer // scans}


def place_of(places_ref, index, block):
    return places_ref[0, index] // block, places_ref[1, index]


def fetch_kernel(
    sizes, places_ref, object_ref, probe_ref, got_ref, squares_ref,
    rows, square, send, recv, send_p, recv_p,
):
    scans, tiles, modes = sizes
    scan, tile, mode = lax.axis_index("scan"), lax.axis_index("tile"), lax.axis_index("mode")
    me = scan * tiles + tile
    barrier, total = greet(
        [
            (me, scans * tiles, functools.partial(pattern_id, tiles)),
            (scan + scans * mode, scans * modes, functools.partial(round_id, scans)),
        ]
    )
    block = object_ref.shape[2]
    columns = object_ref.shape[3]
    rounds, width = rows.shape[1], rows.shape[4]
    for index in range(tiles):
        start, col = place_of(places_ref, scan * tiles + index, block)
        first = (start + lax.rem(tile - start + tiles * block * block, tiles)) // tiles
        piece = object_ref[pl.ds(first, rounds)].reshape(rounds * 2 * block, columns)
        piece = pltpu.roll(piece, lax.rem(columns - col, columns), 1)[:, :width]
        rows[index] = piece.reshape(rounds, 2, block, width)
    share = square.shape[0]
    square[...] = power(probe_ref[pl.ds((scan * tiles + tile) * share, share)])
    pl.semaphore_wait(barrier, total)
    copies = sends(tile, tiles, tile_id, lambda peer: rows.at[peer], got_ref, send, recv)
    copies += sends(mode, modes, mode_id, lambda peer: square, squares_ref, send_p, recv_p)
    got_ref[tile] = rows[tile]
    squares_ref[mode] = square[...]
    for copy in copies:
        copy.wait()


def forward_kernel(
    sizes, places_ref, got_ref, squares_ref, probe_ref, rh, rl, gh, gl,
    window_ref, far_ref, power_ref, square_ref, bright_ref,
):
    width = probe_ref.shape[0]
    block = got_ref.shape[3]
    tiles = sizes[1]
    me = lax.axis_index("scan") * tiles + lax.axis_index("tile")
    start, _ = place_of(places_ref, me, block)
    for index in range(width // block):
        owner = lax.rem(start + index, tiles)
        for part in range(2):
            window_ref[index * block : (index + 1) * block, part * width : (part + 1) * width] = (
                got_ref[owner, index // tiles, part]
            )
    waves = times(probe_ref[...], window_ref[...])
    far = left_product(gh[...], gl[...], right_product(waves, rh[...], rl[...]))
    far_ref[...] = far
    power_ref[...] = power(far).reshape(power_ref.shape)
    square_ref[...] = jnp.sum(squares_ref[...], axis=0)
    bright_ref[...] = power(window_ref[...]).reshape(bright_ref.shape)


def ratio_kernel(
    sizes, power_ref, square_ref, bright_ref, measured_ref, ratio_ref, squares_ref, sum_ref,
    got, got_b, send, recv, send_r, recv_r, send_p, recv_p, send_b, recv_b,
):
    scans, tiles, modes = sizes
    mode = lax.axis_index("mode")
    me = lax.axis_index("scan") * tiles + lax.axis_index("tile")
    id_of = functools.partial(pattern_id, tiles)
    first = sends(mode, modes, mode_id, lambda peer: power_ref.at[peer], got, send, recv)
    other = sends(me, scans * tiles, id_of, lambda peer: square_ref, squares_ref, send_p, recv_p)
    more = sends(
        me, scans * tiles, id_of, lambda peer: bright_ref.at[peer], got_b, send_b, recv_b
    )
    got_b[me] = bright_ref[me]
    got[mode] = power_ref[mode]
    squares_ref[me] = square_ref[...]
    for copy in first:
        copy.wait()
    total = got[0]
    for index in range(1, modes):
        total = total + got[index]
    ratio_ref[mode] = jnp.sqrt(measured_ref[mode] / jnp.maximum(total, floor_level))
    last = sends(
        mode, modes, mode_id, lambda peer: ratio_ref.at[mode], ratio_ref, send_r, recv_r
    )
    for copy in more + other:
        copy.wait()
    sum_ref[...] = jnp.sum(got_b[...], axis=0)
    for copy in last:
        copy.wait()


def inverse_kernel(
    sizes, places_ref, ratio_ref, far_ref, window_ref, probe_ref, rh, rl, gh, gl,
    terms_ref, mixed_ref, ordered,
):
    width = probe_ref.shape[0]
    block = terms_ref.shape[2]
    tiles = sizes[1]
    count = sizes[0] * tiles
    me = lax.axis_index("scan") * tiles + lax.axis_index("tile")
    start, _ = place_of(places_ref, me, block)
    ratio = ratio_ref[...].reshape(width, width)
    scaled = far_ref[...] * jnp.concatenate([ratio, ratio], 1)
    waves = left_product(rh[...], rl[...], right_product(scaled, gh[...], gl[...]))
    probe, window = probe_ref[...], window_ref[...]
    difference = waves - times(probe, window)
    terms = conj_times(probe, difference)
    ordered[...] = terms.reshape(ordered.shape)
    for owner in range(count):
        first = lax.rem(owner - start + count * block * block, count)
        for index in range(terms_ref.shape[1]):
            terms_ref[owner, index] = ordered[first + count * index]
    mixed_ref[...] = difference.reshape(mixed_ref.shape)


def reduce_kernel(
    sizes, places_ref, window_ref, squares_ref,
    terms_ref, mixed_ref, probe_ref, square_ref, bright_ref, object_ref,
    out_ref, next_ref,
    got_t, got_p, canvas, got_c,
    send_t, recv_t, send_m, recv_m, send_c, recv_c, send_o, recv_o, send_n, recv_n,
):
    scans, tiles, modes = sizes
    count = scans * tiles
    rounds, block, width2 = terms_ref.shape[1:]
    width = width2 // 2
    columns = object_ref.shape[-1]
    share = got_p.shape[1]
    scan, tile, mode = lax.axis_index("scan"), lax.axis_index("tile"), lax.axis_index("mode")
    me = scan * tiles + tile
    cycle = scan + scans * mode
    id_of = functools.partial(pattern_id, tiles)
    id_round = functools.partial(round_id, scans)
    moves_t = sends(me, count, id_of, lambda peer: terms_ref.at[peer], got_t, send_t, recv_t)
    got_t[me] = terms_ref[me]
    square_ref[...] = squares_ref[...].reshape(square_ref.shape)
    mixed_ref[...] = conj_times(window_ref[...].reshape(mixed_ref.shape), mixed_ref[...])
    got_p[me] = mixed_ref[me]
    blank = jnp.zeros((block, columns - width), f32)
    zero = jnp.zeros((block, columns), f32)

    def spread(piece, col):
        return pltpu.roll(jnp.concatenate([piece, blank], 1), col, 1)

    weight = zero
    for index in range(count):
        start, col = place_of(places_ref, index, block)
        which = me + count * mode - start
        inside = jnp.logical_and(which >= 0, which < count * rounds)
        piece = square_ref[jnp.clip(which, 0, count * rounds - 1)]
        weight = weight + jnp.where(inside, spread(piece, col), 0.0)
    for copy in moves_t:
        copy.wait()
    moves_p = sends(me, count, id_of, lambda peer: mixed_ref.at[peer], got_p, send_m, recv_m)
    for part in range(2):
        sums = [zero] * modes
        for index in range(count):
            start, col = place_of(places_ref, index, block)
            first = (start + lax.rem(me - start + count * block * block, count)) // count
            for step in range(rounds):
                piece = spread(got_t[index, step, :, part * width : (part + 1) * width], col)
                for slot in range(modes):
                    sums[slot] = sums[slot] + jnp.where(first + step == slot, piece, 0.0)
        for slot in range(modes):
            canvas[slot, part] = sums[slot]
    moves_c = sends(mode, modes, mode_id, lambda peer: canvas.at[peer], got_c, send_c, recv_c)
    got_c[mode] = canvas[mode]
    for copy in moves_c:
        copy.wait()
    for part in range(2):
        total = got_c[0, part]
        for index in range(1, modes):
            total = total + got_c[index, part]
        out_ref[cycle, part] = object_ref[cycle, part] + total / (weight + damping)
    last = sends(
        cycle, scans * modes, id_round, lambda peer: out_ref.at[cycle], out_ref, send_o, recv_o
    )
    for copy in moves_p:
        copy.wait()
    totals = got_p[0]
    for index in range(1, count):
        totals = totals + got_p[index]
    divisor = bright_ref[...]
    next_ref[me] = probe_ref[pl.ds(me * share, share)] + totals / jnp.concatenate([divisor, divisor], 1)
    last += sends(me, count, id_of, lambda peer: next_ref.at[me], next_ref, send_n, recv_n)
    for copy in last:
        copy.wait()


def wave_kernel(
    sizes, places_ref, object_ref, probe_ref, measured_ref, rh, rl, gh, gl, out_ref, next_ref,
    rows, square, got_w, squares_m, window, far, strength, square_m, bright,
    ratio, squares, bright_sum, got_s, got_b, terms, mixed, ordered, squares_b,
    got_t, got_p, canvas, got_c, *sems,
):
    fetch_kernel(
        sizes, places_ref, object_ref, probe_ref, got_w, squares_m, rows, square, *sems[:4]
    )
    forward_kernel(
        sizes, places_ref, got_w, squares_m, probe_ref, rh, rl, gh, gl,
        window, far, strength, square_m, bright,
    )
    ratio_kernel(
        sizes, strength, square_m, bright, measured_ref, ratio, squares, bright_sum,
        got_s, got_b, *sems[4:12],
    )
    inverse_kernel(
        sizes, places_ref, ratio, far, window, probe_ref, rh, rl, gh, gl,
        terms, mixed, ordered,
    )
    reduce_kernel(
        sizes, places_ref, window, squares, terms, mixed, probe_ref, squares_b, bright_sum, object_ref,
        out_ref, next_ref, got_t, got_p, canvas, got_c, *sems[12:],
    )


def shape(*dims):
    return jax.ShapeDtypeStruct(dims, f32)


def dma(count):
    return pltpu.SemaphoreType.DMA((count,))


def one_wave(sizes, tables, object_field, probe_modes, intensities, positions):
    scans, tiles, modes = sizes
    count = scans * tiles
    width = probe_modes.shape[1]
    cycles, _, block, _, columns = object_field.shape
    blocks = width // block
    rounds = blocks // tiles
    parts = blocks // count
    share = width // count
    quarter = width // modes
    planar = jnp.swapaxes(object_field[:, 0], 1, 2)
    buffers = [
        (tiles, rounds, 2, block, width),
        (share, width),
        (tiles, rounds, 2, block, width),
        (modes, share, width),
        (width, 2 * width),
        (width, 2 * width),
        (modes, quarter, width),
        (share, width),
        (count, share, width),
        (modes, quarter, width),
        (count, share, width),
        (share, width),
        (modes, quarter, width),
        (count, share, width),
        (count, parts, block, 2 * width),
        (count, share, 2 * width),
        (blocks, block, 2 * width),
        (blocks, block, width),
        (count, parts, block, 2 * width),
        (count, share, 2 * width),
        (modes, 2, block, columns),
        (modes, 2, block, columns),
    ]
    peers = [tiles] * 2 + [modes] * 6 + [count] * 8 + [modes] * 2 + [cycles] * 2 + [count] * 2
    updated, probe_next = pl.pallas_call(
        functools.partial(wave_kernel, sizes),
        out_shape=[shape(cycles, 2, block, columns), shape(count, share, 2 * width)],
        in_specs=[SMEM] + [VMEM] * 7,
        out_specs=[VMEM] * 2,
        scratch_shapes=[pltpu.VMEM(dims, f32) for dims in buffers]
        + [dma(peer - 1) for peer in peers],
        compiler_params=pltpu.CompilerParams(
            collective_id=0, has_side_effects=True, vmem_limit_bytes=vmem_bytes
        ),
    )(
        positions.T,
        planar,
        probe_modes[0],
        intensities.reshape(modes, quarter, width),
        *tables,
    )
    new_object = jnp.swapaxes(updated, 1, 2)[:, None]
    return (new_object, probe_next.reshape(1, width, 2 * width))


def solution(mesh):
    in_specs = (
        P(None, "tile", None, None, None),
        P("mode", None, None),
        P(("scan", "tile"), None, None),
        P(),
    )
    out_specs = (P(None, "tile", None, None, None), P("mode", None, None))
    sizes = (mesh.shape["scan"], mesh.shape["tile"], mesh.shape["mode"])

    def run(object_field, probe_modes, intensities, positions):
        body = on_device
        if (
            object_field.shape[0] == sizes[0] * sizes[2]
            and probe_modes.shape[0] == sizes[2]
            and intensities.shape[0] == sizes[0] * sizes[1]
            and probe_modes.shape[1] % (object_field.shape[2] * sizes[0] * sizes[1]) == 0
        ):
            tables = [jnp.asarray(table) for table in split_tables(probe_modes.shape[1])]
            body = functools.partial(one_wave, sizes, tables)
        return jax.shard_map(
            body, mesh=mesh, in_specs=in_specs, out_specs=out_specs, check_vma=False
        )(object_field, probe_modes, intensities, positions)

    return run
```
